32 devices in a mesh: date: 2 (over y), trade: 8 (over z, x), path: 2 (over core).
Axes of the slice: x: 2, y: 2, z: 4, core: 2. Of those that a mesh axis runs over, the one named last changes fastest.
Arguments:
- basis_values: bfloat16 [2048, 512], P(('date', 'path')), parts along dimension 0, may hold values from -6 to 6
- coefficients: bfloat16 [2560, 512], P(('date', 'trade')), parts along dimension 0, may hold values from -0.25 to 0.25
- trade_cpty: int32 [1280], P('trade'), may hold values from 0 to 127, as said below
- trade_bucket: int32 [1280], P('trade'), may hold values from 0 to 127
- risk_weights: float32 [128], replicated, may hold values from 0.5 to 2
- correlation: float32 [128, 128], replicated, may hold values from 0 to 1, as said below
- funding_spread: float32 [128], P('trade'), may hold values from 0.5 to 2
Outputs:
- margin: float32 [128, 2048], P('trade', ('date', 'path')), parts along dimension 1
- basis_adjoint: bfloat16 [2048, 512], P(('date', 'path')), parts along dimension 0
The draws below stay inside these ranges and needn't reach their ends.
There are 2 independent parts, one for each index of `date`. The reference program is written for one: setup_inputs(seed, part) draws one part's arguments, and reference() takes and returns one part's arrays. A program takes and returns all parts, laid end to end along the dimension named above; an argument that names none is the same for every part. Nothing has to cross between parts.
Inputs may be any that keep to these rules, and one draw needn't show every extreme that they name: `trade_cpty`: counterparty c belongs to owner block c // 16. Among the trades of one device, at most 40 belong to counterparties of one owner block; in every draw one owner block receives exactly 40 from every device. Counterparties differ in size. `correlation`: symmetric positive definite with unit diagonal; smallest eigenvalue at least 0.01; entries positive.
All inputs are finite; a program needn't handle non-finite values.
Results may differ from the reference program's by a relative error of at most 0.0034.
Values may be sent and summed in bfloat16 or wider, within the bound.
A program may use at most 64 MiB of HBM per device.

```python
import math
import jax
import jax.numpy as jnp
from jax import lax

BASIS = 512
BUCKETS = 128
CP_DEV = 16
TRADE_DEV = 160
CAP = 40
COUNTERPARTIES = 128
TRADES = 1280
PATHS = 1024
N_TRADE = 8


def draw_trade_cpty(key, part):
    slot_total = N_TRADE * CAP
    starred = jax.random.randint(jax.random.fold_in(key, 7), (), 0, N_TRADE)
    shifts = jax.random.randint(jax.random.fold_in(key, 11), (N_TRADE,), 0, CP_DEV)

    def one_device(device_index):
        device_key = jax.random.fold_in(key, device_index + 100)
        ranks = jax.random.permutation(jax.random.fold_in(device_key, 1), slot_total).astype(jnp.int32)
        slot_owner = jnp.arange(slot_total, dtype=jnp.int32) // CAP
        scores = jnp.where(slot_owner == starred, ranks - slot_total, ranks)
        picked = jnp.argsort(scores)[:TRADE_DEV].astype(jnp.int32)
        owner_of = picked // CAP
        first_pick = jax.random.randint(jax.random.fold_in(device_key, 2), (TRADE_DEV,), 0, CP_DEV)
        second_pick = jax.random.randint(jax.random.fold_in(device_key, 3), (TRADE_DEV,), 0, CP_DEV)
        local_cpty = (jnp.minimum(first_pick, second_pick) + shifts[owner_of]) % CP_DEV
        return (owner_of * CP_DEV + local_cpty).astype(jnp.int32)
    return jax.vmap(one_device)(jnp.arange(N_TRADE, dtype=jnp.int32)).reshape(-1).astype(jnp.int32)


def draw_correlation(key, part):
    block_width = 16
    blocks_count = BUCKETS // block_width
    increments = jax.random.randint(jax.random.fold_in(key, 1), (BUCKETS,), 2, 9).astype(jnp.float32)
    tenor_points = jnp.cumsum(increments)
    loading = jax.random.uniform(jax.random.fold_in(key, 2), (blocks_count,), jnp.float32, 0.4, 0.7)
    bucket_ids = jnp.arange(BUCKETS, dtype=jnp.int32)
    currency = bucket_ids // block_width
    common = loading[currency]
    own_part = jnp.sqrt(1.0 - common * common)
    same_block = currency[:, None] == currency[None, :]
    decay_part = jnp.exp(-0.02 * jnp.abs(tenor_points[:, None] - tenor_points[None, :]))
    within = jnp.where(same_block, own_part[:, None] * own_part[None, :] * decay_part, 0.0)
    result = common[:, None] * common[None, :] + within
    diagonal_mask = bucket_ids[:, None] == bucket_ids[None, :]
    return jnp.where(diagonal_mask, 1.0, result).astype(jnp.float32)


def plant(values, rng, smallest, top_value):
    dims = values.shape
    spot = [jax.random.randint(jax.random.fold_in(rng, axis), (), 0, dims[axis]) for axis in range(len(dims))]
    values = values.at[tuple(spot)].set(smallest)
    longest = dims.index(max(dims))
    spot[longest] = (spot[longest] + 1) % dims[longest]
    return values.at[tuple(spot)].set(top_value)


def steps_of(stream_key, dims, split, low, top_value):
    level = 1.0
    for axis_at, shards_of in split:
        heights = jax.random.uniform(jax.random.fold_in(jax.random.fold_in(stream_key, 6), axis_at), (shards_of,), jnp.float32, low / len(split), top_value / len(split))
        level = level * jnp.repeat(jnp.exp(heights), dims[axis_at] // shards_of).reshape((-1,) + (1,) * (len(dims) - 1 - axis_at))
    return level


def gaussian(rng, extent, deviation, bound, cuts=(), held_as=jnp.bfloat16):
    entries = jax.random.normal(rng, extent, jnp.float32) * deviation
    if len(cuts) > 0:
        entries = steps_of(rng, extent, cuts, -0.22, 0.18) * entries
    return jnp.clip(entries, min=-bound, max=bound).astype(held_as)


def setup_inputs(seed: int = 0, part: int = 0) -> dict:
    splits = jax.random.split(jax.random.key(seed), 8)
    part_keys = jax.random.split(jax.random.fold_in(splits[7], part), 8)
    basis_values = gaussian(part_keys[0], (PATHS, BASIS), 1.0, 6.0, ((0, 2),))
    coefficients = gaussian(part_keys[1], (TRADES, BASIS), BASIS ** -0.5, 0.25, ((0, 8),))
    trade_cpty = draw_trade_cpty(jax.random.fold_in(splits[7], 71), part)
    trade_bucket = plant(jax.random.randint(splits[3], (TRADES,), 0, BUCKETS), jax.random.fold_in(splits[3], 1), 0, BUCKETS - 1).astype(jnp.int32)
    risk_weights = jnp.clip(jnp.exp(jax.random.uniform(splits[4], (BUCKETS,), jnp.float32, math.log(0.5), math.log(2.0))), 0.5, 2.0)
    correlation = draw_correlation(jax.random.fold_in(splits[7], 71), part)
    funding_spread = jnp.clip(jnp.exp(math.log(2.0) - 1.3862944 * jax.random.uniform(splits[6], (COUNTERPARTIES,), jnp.float32) ** steps_of(splits[6], (COUNTERPARTIES,), ((0, 8),), -0.2, 0.2)), 0.5, 2.0)
    return dict(basis_values=basis_values, coefficients=coefficients, trade_cpty=trade_cpty, trade_bucket=trade_bucket, risk_weights=risk_weights, correlation=correlation, funding_spread=funding_spread)


def reference(basis_values, coefficients, trade_cpty, trade_bucket, risk_weights, correlation, funding_spread):
    block_rows = 256 if PATHS % 256 == 0 else PATHS
    blocks_count = PATHS // block_rows
    trade_code = (trade_cpty * BUCKETS + trade_bucket).astype(jnp.int32)
    path_blocks = basis_values.reshape(blocks_count, block_rows, BASIS)

    def one_block(basis_block):
        delta_rows = jnp.dot(basis_block, coefficients.T, preferred_element_type=jnp.float32).astype(jnp.bfloat16)
        sens_flat = jax.ops.segment_sum(delta_rows.T.astype(jnp.float32), trade_code, num_segments=COUNTERPARTIES * BUCKETS)
        sens = sens_flat.reshape(COUNTERPARTIES, BUCKETS, block_rows)
        weighted = sens * risk_weights[None, :, None]
        rho_w = jnp.einsum('cbp,db->cdp', weighted, correlation, precision=lax.Precision.HIGHEST)
        margin_now = jnp.sqrt(lax.optimization_barrier(jnp.sum(weighted * rho_w, axis=1)) + 1e-06)
        sens_bar = funding_spread[:, None, None] * risk_weights[None, :, None] * rho_w / margin_now[:, None, :]
        delta_bar = sens_bar.reshape(COUNTERPARTIES * BUCKETS, block_rows)[trade_code].astype(jnp.bfloat16)
        adjoint_rows = jnp.dot(delta_bar.T, coefficients, preferred_element_type=jnp.float32).astype(jnp.bfloat16)
        return (margin_now, adjoint_rows)
    margin_blocks, adjoint_blocks = lax.map(one_block, path_blocks)
    margin = jnp.transpose(margin_blocks, (1, 0, 2)).reshape(COUNTERPARTIES, PATHS)
    basis_adjoint = adjoint_blocks.reshape(PATHS, BASIS)
    return (margin, basis_adjoint)
```

```python
import functools
import jax
import jax.numpy as jnp
from jax import lax
from jax.experimental import pallas as pl
from jax.experimental.pallas import tpu as pltpu
from jax.sharding import PartitionSpec as P

MESH = pl.DeviceIdType.MESH
TERMS = 3
DEEP = 4


def split_terms(value, count):
    parts = []
    for _ in range(count):
        head = value.astype(jnp.bfloat16)
        parts.append(head)
        value = value - head.astype(jnp.float32)
    return parts


def dot_nt(a, b):
    return lax.dot_general(a, b, (((1,), (1,)), ((), ())), preferred_element_type=jnp.float32)


def dot_nn(a, b):
    return jnp.dot(a, b, preferred_element_type=jnp.float32)


def margin_kernel(
    owners, basis_ref, coef_ref, msg_ref, rw_ref, corr_ref,
    adj_ref, margin_ref,
    held, msgs, rows_buf, gram, cols_buf, bucket_hot, cpty_hot, delta_buf, v_buf, bar_buf,
    msend, mrecv,
    base_sem, zu, zd, zr, xs, xr, cs, cr, gs, gr, ms, mr, az_u, az_d, az_r, ax_s, ax_r,
):
    t = lax.axis_index("trade")
    k = lax.axis_index("path")
    z = t // 2
    x = t % 2
    per_device = coef_ref.shape[0]
    half = per_device // 2
    buckets = corr_ref.shape[0]
    trades = owners * per_device
    side = trades // 2
    path_share = rows_buf.shape[0]
    cpty_dev = mrecv.shape[1]
    cptys = owners * cpty_dev

    def slot(zz, xx):
        return xx * DEEP + zz

    def send(src, dst, send_sem, recv_sem, to_trade, to_path):
        return pltpu.make_async_remote_copy(
            src_ref=src, dst_ref=dst, send_sem=send_sem, recv_sem=recv_sem,
            device_id={"trade": to_trade, "path": to_path}, device_id_type=MESH,
        )

    base_copy = pltpu.make_async_copy(
        basis_ref.at[pl.ds(t * path_share, path_share)], rows_buf, base_sem
    )
    base_copy.start()

    barrier = pltpu.get_barrier_semaphore()
    for step in range(1, owners):
        pl.semaphore_signal(
            barrier, inc=1, device_id={"trade": (t + step) % owners, "path": k}, device_id_type=MESH
        )
    pl.semaphore_signal(barrier, inc=1, device_id={"trade": t, "path": 1 - k}, device_id_type=MESH)
    pl.semaphore_wait(barrier, owners)

    def msg_copy(step):
        return send(
            msg_ref, msgs.at[step], gs.at[step], gr.at[step], (t + step) % owners, k
        )

    for step in range(1, owners):
        msg_copy(step).start()

    def own_half():
        return coef_ref.at[pl.ds(pl.multiple_of(k * half, 16), half)]

    def held_at(zz, xx, kk):
        return held.at[slot(zz, xx) * 2 + kk]

    def up(zz, src):
        return send(src, held_at(zz, x, k), zu.at[zz], zr.at[zz], (z + 1) * 2 + x, k)

    def down(zz, src):
        return send(src, held_at(zz, x, k), zd.at[zz], zr.at[zz], (z - 1) * 2 + x, k)

    def across(zz, src):
        return send(src, held_at(zz, x, k), xs.at[zz], xr.at[zz], z * 2 + 1 - x, k)

    def over(zz, xx):
        where = slot(zz, xx)
        return send(held_at(zz, xx, k), held_at(zz, xx, k), cs.at[where], cr.at[where], t, 1 - k)

    @pl.when(z < DEEP - 1)
    def _():
        up(z, own_half()).start()

    @pl.when(z > 0)
    def _():
        down(z, own_half()).start()

    across(z, own_half()).start()

    held[slot(z, x) * 2] = coef_ref[:half]
    held[slot(z, x) * 2 + 1] = coef_ref[half:]

    def chain_arrival(j):
        @pl.when(z - j >= 0)
        def _():
            zz = z - j
            src = held_at(zz, x, k)
            up(zz, src).wait_recv()

            @pl.when(z < DEEP - 1)
            def _():
                up(zz, src).start()
            across(zz, src).start()
            over(zz, x).start()

        @pl.when(z + j < DEEP)
        def _():
            zz = z + j
            src = held_at(zz, x, k)
            down(zz, src).wait_recv()

            @pl.when(z > 0)
            def _():
                down(zz, src).start()
            across(zz, src).start()
            over(zz, x).start()

    def across_at(zz):
        across(zz, held_at(zz, 1 - x, k)).wait_recv()
        over(zz, 1 - x).start()

    def across_arrival(j):
        if j == 0:
            across_at(z)
            return

        @pl.when(z - j >= 0)
        def _():
            across_at(z - j)

        @pl.when(z + j < DEEP)
        def _():
            across_at(z + j)

    rw_rows = jnp.broadcast_to(rw_ref[...], (buckets, buckets))
    scaled = corr_ref[...] * rw_rows * rw_rows.T
    scaled_terms = split_terms(scaled, TERMS)

    for step in range(1, owners):
        msg_copy(step).wait_recv()
    total = msg_ref[...]
    for step in range(1, owners):
        total = total + msgs[step]
    spread = total[:, trades:trades + cptys]
    codes = total[:, :trades].astype(jnp.int32)
    cpty_row = codes // buckets
    bucket_row = codes % buckets
    bucket_hot[...] = (
        lax.broadcasted_iota(jnp.int32, (buckets, trades), 0) == bucket_row
    ).astype(jnp.float32).astype(jnp.bfloat16)
    cpty_hot[...] = (
        lax.broadcasted_iota(jnp.int32, (cptys, trades), 0) == cpty_row
    ).astype(jnp.float32).astype(jnp.bfloat16)
    cols_buf[...] = jnp.broadcast_to(codes.astype(jnp.float32), (8, trades)).T.astype(jnp.int32)

    def build(first, last):
        @pl.loop(first, last)
        def _(i):
            rows = pl.ds(pl.multiple_of(i * per_device, 16), per_device)
            code_col = cols_buf[rows, :1]
            hot = (
                lax.broadcasted_iota(jnp.int32, (per_device, buckets), 1) == code_col % buckets
            ).astype(jnp.float32).astype(jnp.bfloat16)
            same = code_col // buckets == cpty_row
            for term in range(TERMS):
                picked = dot_nn(hot, scaled_terms[term]).astype(jnp.bfloat16)
                block = dot_nn(picked, bucket_hot[...])
                gram[term, rows, :] = jnp.where(same, block, 0.0).astype(jnp.bfloat16)

    def deltas(group):
        lanes = pl.ds(pl.multiple_of(group * side, 128), side)
        rows = pl.ds(pl.multiple_of(group * side, 128), side)
        coef_rows = held[pl.ds(group * owners, owners)].reshape(side, coef_ref.shape[1])
        delta = dot_nt(rows_buf[...], coef_rows).astype(jnp.bfloat16)
        delta_buf[:, lanes] = delta
        out = dot_nn(delta, gram[TERMS - 1, rows, :])
        for term in range(TERMS - 2, -1, -1):
            out = out + dot_nn(delta, gram[term, rows, :])
        return out

    def over_arrivals(xx, skip_own):
        for zz in range(DEEP):
            if skip_own:
                @pl.when(zz != z)
                def _():
                    over(zz, xx).wait_recv()
            else:
                over(zz, xx).wait_recv()

    build(0, 2)
    chain_arrival(1)
    across_arrival(0)
    build(2, 4)
    chain_arrival(2)
    across_arrival(1)
    build(4, 6)
    chain_arrival(3)
    build(6, 8)
    base_copy.wait()
    over_arrivals(x, True)
    v_buf[...] = deltas(x)
    across_arrival(2)
    across_arrival(3)
    over_arrivals(1 - x, False)
    v = v_buf[...] + deltas(1 - x)

    terms = jnp.concatenate(split_terms(delta_buf[...].astype(jnp.float32) * v, 3), axis=0)
    sums = dot_nt(terms, cpty_hot[...])
    quad = sums[:path_share] + (sums[path_share:2 * path_share] + sums[2 * path_share:])
    margin = jnp.sqrt(quad + 1e-06)
    ratio_terms = jnp.concatenate(split_terms(spread / margin, 3), axis=0)
    spans = dot_nn(ratio_terms, cpty_hot[...])
    ratio = spans[:path_share] + (spans[path_share:2 * path_share] + spans[2 * path_share:])
    bar_buf[...] = (ratio * v).astype(jnp.bfloat16)
    flipped = jnp.concatenate([margin, margin], axis=0).T[:, :path_share]
    msend[...] = flipped.reshape(owners, cpty_dev, path_share)

    def margin_copy(step):
        to = (t + step) % owners
        return send(msend.at[to], mrecv.at[step], ms.at[step], mr.at[step], to, k)

    for step in range(1, owners):
        margin_copy(step).start()

    coef_all = held[...].reshape(trades, coef_ref.shape[1])
    adj_ref[t] = dot_nn(bar_buf[...], coef_all).astype(jnp.bfloat16)

    def a_up(zz):
        ref = adj_ref.at[zz * 2 + x]
        return send(ref, ref, az_u.at[zz], az_r.at[zz], (z + 1) * 2 + x, k)

    def a_down(zz):
        ref = adj_ref.at[zz * 2 + x]
        return send(ref, ref, az_d.at[zz], az_r.at[zz], (z - 1) * 2 + x, k)

    def a_across(zz, xx):
        ref = adj_ref.at[zz * 2 + xx]
        return send(ref, ref, ax_s.at[zz], ax_r.at[zz], z * 2 + 1 - x, k)

    @pl.when(z < DEEP - 1)
    def _():
        a_up(z).start()

    @pl.when(z > 0)
    def _():
        a_down(z).start()

    a_across(z, x).start()
    for j in range(1, DEEP):
        @pl.when(z - j >= 0)
        def _():
            a_up(z - j).wait_recv()

            @pl.when(z < DEEP - 1)
            def _():
                a_up(z - j).start()
            a_across(z - j, x).start()

        @pl.when(z + j < DEEP)
        def _():
            a_down(z + j).wait_recv()

            @pl.when(z > 0)
            def _():
                a_down(z + j).start()
            a_across(z + j, x).start()

    for step in range(1, owners):
        margin_copy(step).wait_recv()
    mrecv[0] = msend[t]
    for first in range(0, owners, 2):
        pair = [mrecv[(t - sender) % owners] for sender in (first, first + 1)]
        margin_ref[:, first * path_share:(first + 2) * path_share] = jnp.concatenate(pair, axis=1)

    for zz in range(DEEP):
        a_across(zz, 1 - x).wait_recv()

    for step in range(1, owners):
        msg_copy(step).wait_send()
        margin_copy(step).wait_send()
    for zz in range(DEEP):
        across(zz, own_half()).wait_send()
        a_across(zz, x).wait_send()
        over(zz, 1 - x).wait_send()

        @pl.when(zz != z)
        def _():
            over(zz, x).wait_send()

        @pl.when((zz <= z) & (z < DEEP - 1))
        def _():
            up(zz, own_half()).wait_send()
            a_up(zz).wait_send()

        @pl.when((zz >= z) & (z > 0))
        def _():
            down(zz, own_half()).wait_send()
            a_down(zz).wait_send()


def split_paths(
    basis_values, coefficients, trade_cpty, trade_bucket, risk_weights, correlation, funding_spread
):
    owners = lax.axis_size("trade")
    per_device, width = coefficients.shape
    cpty_dev = funding_spread.shape[0]
    buckets = risk_weights.shape[0]
    path_rows = basis_values.shape[0]
    path_share = path_rows // owners
    trades = owners * per_device
    cptys = owners * cpty_dev
    t = lax.axis_index("trade")
    place = (t % 2 * DEEP + t // 2) * per_device
    codes = (trade_cpty * buckets + trade_bucket).astype(jnp.float32)
    msg = jnp.zeros((1, trades + cptys), jnp.float32)
    msg = lax.dynamic_update_slice(msg, codes[None, :], (0, place))
    msg = lax.dynamic_update_slice(msg, funding_spread[None, :], (0, trades + t * cpty_dev))
    vmem = pl.BlockSpec(memory_space=pltpu.VMEM)
    dma = pltpu.SemaphoreType.DMA
    adj, margin = pl.pallas_call(
        functools.partial(margin_kernel, owners),
        out_shape=(
            jax.ShapeDtypeStruct((owners, path_share, width), jnp.bfloat16),
            jax.ShapeDtypeStruct((cpty_dev, path_rows), jnp.float32),
        ),
        in_specs=[pl.BlockSpec(memory_space=pl.ANY)] + [vmem] * 4,
        out_specs=(vmem, vmem),
        scratch_shapes=[
            pltpu.VMEM((owners * 2, per_device // 2, width), jnp.bfloat16),
            pltpu.VMEM((owners, 1, trades + cptys), jnp.float32),
            pltpu.VMEM((path_share, width), jnp.bfloat16),
            pltpu.VMEM((TERMS, trades, trades), jnp.bfloat16),
            pltpu.VMEM((trades, 8), jnp.int32),
            pltpu.VMEM((buckets, trades), jnp.bfloat16),
            pltpu.VMEM((cptys, trades), jnp.bfloat16),
            pltpu.VMEM((path_share, trades), jnp.bfloat16),
            pltpu.VMEM((path_share, trades), jnp.float32),
            pltpu.VMEM((path_share, trades), jnp.bfloat16),
            pltpu.VMEM((owners, cpty_dev, path_share), jnp.float32),
            pltpu.VMEM((owners, cpty_dev, path_share), jnp.float32),
            dma, dma((DEEP,)), dma((DEEP,)), dma((DEEP,)), dma((DEEP,)), dma((DEEP,)),
            dma((owners,)), dma((owners,)), dma((owners,)), dma((owners,)),
            dma((owners,)), dma((owners,)),
            dma((DEEP,)), dma((DEEP,)), dma((DEEP,)), dma((DEEP,)), dma((DEEP,)),
        ],
        compiler_params=pltpu.CompilerParams(
            collective_id=0, has_side_effects=True, vmem_limit_bytes=40 * 1024 * 1024
        ),
    )(basis_values, coefficients, msg, risk_weights[None, :], correlation)
    return (margin, adj.reshape(path_rows, width))


def margin_terms(arrived, got_codes, risk_weights, correlation, funding_spread):
    path_rows = arrived.shape[0]
    cpty_count = funding_spread.shape[0]
    bucket_count = risk_weights.shape[0]
    is_filled = got_codes >= 0
    column_ids = jnp.arange(cpty_count * bucket_count, dtype=jnp.int32)
    hot_table = (got_codes[:, None] == column_ids[None, :]).astype(jnp.bfloat16)
    bucket_sums = jnp.dot(arrived, hot_table, preferred_element_type=jnp.float32)
    weighted = (
        bucket_sums.reshape(path_rows, cpty_count, bucket_count) * risk_weights[None, None, :]
    )
    rho_w = jnp.einsum("pcb,db->pcd", weighted, correlation, precision=lax.Precision.HIGHEST)
    margin_now = jnp.sqrt(jnp.sum(weighted * rho_w, axis=2) + 1e-06)
    sens_bar = (
        funding_spread[None, :, None] * risk_weights[None, None, :] * rho_w / margin_now[:, :, None]
    )
    flat_bar = sens_bar.reshape(path_rows, cpty_count * bucket_count)
    safe_codes = jnp.where(is_filled, got_codes, 0)
    slot_bar = jnp.take(flat_bar, safe_codes, axis=1) * is_filled[None, :].astype(jnp.float32)
    return (margin_now, slot_bar.astype(jnp.bfloat16))


def body(
    basis_values, coefficients, trade_cpty, trade_bucket, risk_weights, correlation, funding_spread
):
    owners = lax.axis_size("trade")
    per_device = coefficients.shape[0]
    capacity = max(2, 2 * per_device // owners)
    slot_total = owners * capacity
    cpty_count = funding_spread.shape[0]
    bucket_count = risk_weights.shape[0]
    path_rows = basis_values.shape[0]
    owner_of = trade_cpty // cpty_count
    trade_code = trade_cpty % cpty_count * bucket_count + trade_bucket
    position = jnp.arange(per_device, dtype=jnp.int32)
    same_owner = owner_of[:, None] == owner_of[None, :]
    earlier = position[None, :] < position[:, None]
    rank_in = jnp.sum((same_owner & earlier).astype(jnp.int32), axis=1)
    slot_index = owner_of * capacity + rank_in
    codes_out = jnp.full((slot_total,), -1, jnp.int32).at[slot_index].set(trade_code)
    got_codes = lax.all_to_all(codes_out, "trade", split_axis=0, concat_axis=0, tiled=True)
    delta_rows = lax.dot_general(
        basis_values, coefficients, (((1,), (1,)), ((), ())), preferred_element_type=jnp.float32
    ).astype(jnp.bfloat16)
    outgoing = jnp.zeros((path_rows, slot_total), jnp.bfloat16).at[:, slot_index].set(delta_rows)
    arrived = lax.all_to_all(outgoing, "trade", split_axis=1, concat_axis=1, tiled=True)
    margin_now, slot_bar = margin_terms(
        arrived, got_codes, risk_weights, correlation, funding_spread
    )
    returned = lax.all_to_all(slot_bar, "trade", split_axis=1, concat_axis=1, tiled=True)
    delta_bar = returned[:, slot_index]
    partial_adj = jnp.dot(delta_bar, coefficients, preferred_element_type=jnp.float32)
    basis_adjoint = lax.psum(partial_adj, "trade").astype(jnp.bfloat16)
    return (margin_now.T, basis_adjoint)


def solution(mesh):
    placed = (
        P(("date", "path"), None),
        P(("date", "trade"), None),
        P("trade"),
        P("trade"),
        P(),
        P(),
        P("trade"),
    )
    whole = split_paths if mesh.shape["trade"] == 2 * DEEP else body
    return jax.shard_map(
        whole,
        mesh=mesh,
        in_specs=placed,
        out_specs=(P("trade", ("date", "path")), P(("date", "path"), None)),
        check_vma=False,
    )
```

```python
import functools
import jax
import jax.numpy as jnp
from jax import lax
from jax.experimental import pallas as pl
from jax.experimental.pallas import tpu as pltpu
from jax.sharding import PartitionSpec as P

MESH = pl.DeviceIdType.MESH
TERMS = 2
PIECES = 2
DEEP = 4


def split_terms(value, count):
    parts = []
    for _ in range(count):
        head = value.astype(jnp.bfloat16)
        parts.append(head)
        value = value - head.astype(jnp.float32)
    return parts


def dot_nt(a, b):
    return lax.dot_general(a, b, (((1,), (1,)), ((), ())), preferred_element_type=jnp.float32)


def dot_nn(a, b):
    return jnp.dot(a, b, preferred_element_type=jnp.float32)


def margin_kernel(
    owners, basis_in, coef_in, cpty_in, bucket_in, rw_in, corr_in, spread_in,
    adj_ref, margin_ref,
    held, rows_buf, cpty_buf, bucket_buf, rw_buf, corr_buf, spread_buf,
    msg, msgs, gram, cols_buf, bucket_hot, cpty_hot, bar_buf, msend, mrecv,
    local, zu, zd, zr, xs, xr, cs, cr, gs, gr, ms, mr, az_u, az_d, az_r, ax_s, ax_r,
):
    t = lax.axis_index("trade")
    k = lax.axis_index("path")
    z = t // 2
    x = t % 2
    per_device, width = coef_in.shape
    half = per_device // 2
    span = width // PIECES
    buckets = corr_in.shape[0]
    trades = owners * per_device
    path_share = rows_buf.shape[0]
    cpty_dev = mrecv.shape[1]
    cptys = owners * cpty_dev
    code_lanes = -(-per_device // 128) * 128

    def slot(zz, xx, rz, rx):
        return (xx + rx) % 2 * 4 + (zz // 2 + rz // 2) % 2 * 2 + zz % 2

    def send(src, dst, send_sem, recv_sem, to_trade, to_path):
        return pltpu.make_async_remote_copy(
            src_ref=src, dst_ref=dst, send_sem=send_sem, recv_sem=recv_sem,
            device_id={"trade": to_trade, "path": to_path}, device_id_type=MESH,
        )

    own = slot(z, x, z, x)
    small = [
        pltpu.make_async_copy(cpty_in, cpty_buf, local.at[0]),
        pltpu.make_async_copy(bucket_in, bucket_buf, local.at[1]),
        pltpu.make_async_copy(spread_in, spread_buf, local.at[2]),
    ]
    shard = [
        pltpu.make_async_copy(
            coef_in.at[pl.ds(kk * half, half)], held.at[own * 2 + kk], local.at[3 + kk]
        )
        for kk in range(2)
    ]
    rest = [
        pltpu.make_async_copy(rw_in, rw_buf, local.at[5]),
        pltpu.make_async_copy(corr_in, corr_buf, local.at[6]),
        pltpu.make_async_copy(
            basis_in.at[pl.ds(pl.multiple_of(t * path_share, 16), path_share)], rows_buf, local.at[7]
        ),
    ]
    for copy in small + shard + rest:
        copy.start()

    barrier = pltpu.get_barrier_semaphore()
    for step in range(1, owners):
        pl.semaphore_signal(
            barrier, inc=1, device_id={"trade": (t + step) % owners, "path": k}, device_id_type=MESH
        )
    pl.semaphore_signal(barrier, inc=1, device_id={"trade": t, "path": 1 - k}, device_id_type=MESH)

    for copy in small:
        copy.wait()
    msg[...] = jnp.zeros_like(msg)
    msg[:, :per_device] = (cpty_buf[...] * buckets + bucket_buf[...]).astype(jnp.float32)
    msg[:, code_lanes:code_lanes + cpty_dev] = spread_buf[...]
    msgs[0] = msg[...]
    for copy in shard:
        copy.wait()
    pl.semaphore_wait(barrier, owners)

    def msg_copy(step):
        return send(msg, msgs.at[step], gs.at[step], gr.at[step], (t + step) % owners, k)

    for step in range(1, owners):
        msg_copy(step).start()

    def piece(where, p):
        return held.at[where * 2 + k, :, pl.ds(p * span, span)]

    def hop(zz, xx, p, sems, arrive, rz, rx):
        return send(
            piece(slot(zz, xx, z, x), p), piece(slot(zz, xx, rz, rx), p),
            sems.at[zz * PIECES + p], arrive.at[zz * PIECES + p], rz * 2 + rx, k,
        )

    def up(zz, p):
        return hop(zz, x, p, zu, zr, z + 1, x)

    def down(zz, p):
        return hop(zz, x, p, zd, zr, z - 1, x)

    def across(zz, p):
        return hop(zz, x, p, xs, xr, z, 1 - x)

    def over(where, p):
        ref = piece(where, p)
        sem = where * PIECES + p
        return send(ref, ref, cs.at[sem], cr.at[sem], t, 1 - k)

    def chain_arrived(zz, p):
        ref = piece(slot(zz, x, z, x), p)
        sem = zz * PIECES + p
        send(ref, ref, zu.at[sem], zr.at[sem], z * 2 + 1 - x, k).wait_recv()

    def across_arrived(zz, p):
        ref = piece(slot(zz, 1 - x, z, x), p)
        sem = zz * PIECES + p
        send(ref, ref, xs.at[sem], xr.at[sem], z * 2 + 1 - x, k).wait_recv()

    for p in range(PIECES):
        @pl.when(z < DEEP - 1)
        def _():
            up(z, p).start()

        @pl.when(z > 0)
        def _():
            down(z, p).start()

        across(z, p).start()

    def chain_arrival(j, p):
        @pl.when(z - j >= 0)
        def _():
            zz = z - j
            chain_arrived(zz, p)

            @pl.when(z < DEEP - 1)
            def _():
                up(zz, p).start()
            across(zz, p).start()
            over(slot(zz, x, z, x), p).start()

        @pl.when(z + j < DEEP)
        def _():
            zz = z + j
            chain_arrived(zz, p)

            @pl.when(z > 0)
            def _():
                down(zz, p).start()
            across(zz, p).start()
            over(slot(zz, x, z, x), p).start()

    def across_at(zz, p):
        across_arrived(zz, p)
        over(slot(zz, 1 - x, z, x), p).start()

    def across_arrival(j, p):
        if j == 0:
            across_at(z, p)
            return

        @pl.when(z - j >= 0)
        def _():
            across_at(z - j, p)

        @pl.when(z + j < DEEP)
        def _():
            across_at(z + j, p)

    for copy in rest:
        copy.wait()
    rw_rows = jnp.broadcast_to(rw_buf[...], (buckets, buckets))
    scaled = corr_buf[...] * rw_rows * rw_rows.T
    scaled_terms = split_terms(scaled, TERMS)

    chain_arrival(1, 0)
    for step in range(1, owners):
        msg_copy(step).wait_recv()

    def sender(i):
        zz = (i // 2 + z // 2) % 2 * 2 + i % 2
        return zz * 2 + (i // 4 + x) % 2

    codes = jnp.concatenate(
        [msgs[(t - sender(i)) % owners][:, :per_device] for i in range(owners)], axis=1
    ).astype(jnp.int32)
    spread = jnp.concatenate(
        [msgs[(t - o) % owners][:, code_lanes:code_lanes + cpty_dev] for o in range(owners)], axis=1
    )
    cpty_row = codes // buckets
    bucket_row = codes % buckets
    bucket_hot[...] = (
        lax.broadcasted_iota(jnp.int32, (buckets, trades), 0) == bucket_row
    ).astype(jnp.float32).astype(jnp.bfloat16)
    cpty_hot[...] = (
        lax.broadcasted_iota(jnp.int32, (cptys, trades), 0) == cpty_row
    ).astype(jnp.float32).astype(jnp.bfloat16)
    cols_buf[...] = jnp.broadcast_to(codes.astype(jnp.float32), (8, trades)).T.astype(jnp.int32)

    def build(first, last):
        @pl.loop(first, last)
        def _(i):
            rows = pl.ds(pl.multiple_of(i * per_device, 16), per_device)
            code_col = cols_buf[rows, :1]
            hot = (
                lax.broadcasted_iota(jnp.int32, (per_device, buckets), 1) == code_col % buckets
            ).astype(jnp.float32).astype(jnp.bfloat16)
            same = code_col // buckets == cpty_row
            for term in range(TERMS):
                picked = dot_nn(hot, scaled_terms[term]).astype(jnp.bfloat16)
                block = dot_nn(picked, bucket_hot[...])
                gram[term, rows, :] = jnp.where(same, block, 0.0).astype(jnp.bfloat16)

    def deltas(pair):
        for where in (2 * pair, 2 * pair + 1):
            for p in range(PIECES):
                if pair == 0:
                    @pl.when(where != own)
                    def _():
                        over(where, p).wait_recv()
                else:
                    over(where, p).wait_recv()
        rows = slice(pair * 2 * per_device, (pair + 1) * 2 * per_device)
        coef_rows = held[pair * 4:pair * 4 + 4].reshape(2 * per_device, width)
        delta = dot_nt(rows_buf[...], coef_rows).astype(jnp.bfloat16)
        out = dot_nn(delta, gram[TERMS - 1, rows, :])
        for term in range(TERMS - 2, -1, -1):
            out = out + dot_nn(delta, gram[term, rows, :])
        return delta.astype(jnp.float32), out

    across_arrival(0, 0)
    chain_arrival(1, 1)
    across_arrival(0, 1)
    build(0, 1)
    chain_arrival(2, 0)
    build(1, 2)
    chain_arrival(2, 1)
    build(2, 3)
    across_arrival(1, 0)
    chain_arrival(3, 0)
    build(3, 4)
    across_arrival(1, 1)
    chain_arrival(3, 1)
    build(4, 8)
    across_arrival(2, 0)
    across_arrival(2, 1)
    d0, v0 = deltas(0)
    d1, v1 = deltas(1)
    across_arrival(3, 0)
    across_arrival(3, 1)
    d2, v2 = deltas(2)
    early = v0 + v1 + v2
    d3, v3 = deltas(3)
    v = early + v3

    delta_all = jnp.concatenate([d0, d1, d2, d3], axis=1)
    terms = jnp.concatenate(split_terms(delta_all * v, 3), axis=0)
    sums = dot_nt(terms, cpty_hot[...])
    quad = sums[:path_share] + (sums[path_share:2 * path_share] + sums[2 * path_share:])
    margin = jnp.sqrt(quad + 1e-06)
    ratio_terms = jnp.concatenate(split_terms(spread / margin, 3), axis=0)
    spans = dot_nn(ratio_terms, cpty_hot[...])
    ratio = spans[:path_share] + (spans[path_share:2 * path_share] + spans[2 * path_share:])
    bar_buf[...] = (ratio * v).astype(jnp.bfloat16)
    coef_all = held[...].reshape(trades, width)
    adj_ref[t] = dot_nn(bar_buf[...], coef_all).astype(jnp.bfloat16)

    def a_piece(zz, xx, p):
        return adj_ref.at[zz * 2 + xx, :, pl.ds(p * span, span)]

    def a_up(zz, p):
        ref = a_piece(zz, x, p)
        sem = zz * PIECES + p
        return send(ref, ref, az_u.at[sem], az_r.at[sem], (z + 1) * 2 + x, k)

    def a_down(zz, p):
        ref = a_piece(zz, x, p)
        sem = zz * PIECES + p
        return send(ref, ref, az_d.at[sem], az_r.at[sem], (z - 1) * 2 + x, k)

    def a_across(zz, xx, p):
        ref = a_piece(zz, xx, p)
        sem = zz * PIECES + p
        return send(ref, ref, ax_s.at[sem], ax_r.at[sem], z * 2 + 1 - x, k)

    for p in range(PIECES):
        @pl.when(z < DEEP - 1)
        def _():
            a_up(z, p).start()

        @pl.when(z > 0)
        def _():
            a_down(z, p).start()

        a_across(z, x, p).start()

    flipped = jnp.concatenate([margin, margin], axis=0).T[:, :path_share]
    msend[...] = flipped.reshape(owners, cpty_dev, path_share)

    def margin_copy(step):
        to = (t + step) % owners
        return send(msend.at[to], mrecv.at[step], ms.at[step], mr.at[step], to, k)

    for step in range(1, owners):
        margin_copy(step).start()

    for j in range(1, DEEP):
        for p in range(PIECES):
            @pl.when(z - j >= 0)
            def _():
                a_up(z - j, p).wait_recv()

                @pl.when(z < DEEP - 1)
                def _():
                    a_up(z - j, p).start()
                a_across(z - j, x, p).start()

            @pl.when(z + j < DEEP)
            def _():
                a_down(z + j, p).wait_recv()

                @pl.when(z > 0)
                def _():
                    a_down(z + j, p).start()
                a_across(z + j, x, p).start()

    for step in range(1, owners):
        margin_copy(step).wait_recv()
    mrecv[0] = msend[t]
    for first in range(0, owners, 2):
        pair = [mrecv[(t - o) % owners] for o in (first, first + 1)]
        margin_ref[:, first * path_share:(first + 2) * path_share] = jnp.concatenate(pair, axis=1)

    for zz in range(DEEP):
        for p in range(PIECES):
            a_across(zz, 1 - x, p).wait_recv()

    for step in range(1, owners):
        msg_copy(step).wait_send()
        margin_copy(step).wait_send()
    for p in range(PIECES):
        for where in range(owners):
            @pl.when(where != own)
            def _():
                over(where, p).wait_send()
        for zz in range(DEEP):
            across(zz, p).wait_send()
            a_across(zz, x, p).wait_send()

            @pl.when((zz <= z) & (z < DEEP - 1))
            def _():
                up(zz, p).wait_send()
                a_up(zz, p).wait_send()

            @pl.when((zz >= z) & (z > 0))
            def _():
                down(zz, p).wait_send()
                a_down(zz, p).wait_send()


def split_paths(
    basis_values, coefficients, trade_cpty, trade_bucket, risk_weights, correlation, funding_spread
):
    owners = lax.axis_size("trade")
    per_device, width = coefficients.shape
    cpty_dev = funding_spread.shape[0]
    buckets = risk_weights.shape[0]
    path_rows = basis_values.shape[0]
    path_share = path_rows // owners
    trades = owners * per_device
    cptys = owners * cpty_dev
    vmem = pl.BlockSpec(memory_space=pltpu.VMEM)
    hbm = pl.BlockSpec(memory_space=pltpu.HBM)
    dma = pltpu.SemaphoreType.DMA
    f32, i32, bf16 = jnp.float32, jnp.int32, jnp.bfloat16
    msg_lanes = -(-per_device // 128) * 128 + 128
    pieces = DEEP * PIECES
    adj, margin = pl.pallas_call(
        functools.partial(margin_kernel, owners),
        out_shape=(
            jax.ShapeDtypeStruct((owners, path_share, width), bf16),
            jax.ShapeDtypeStruct((cpty_dev, path_rows), f32),
        ),
        in_specs=[hbm] * 7,
        out_specs=(vmem, vmem),
        scratch_shapes=[
            pltpu.VMEM((owners * 2, per_device // 2, width), bf16),
            pltpu.VMEM((path_share, width), bf16),
            pltpu.VMEM((1, per_device), i32),
            pltpu.VMEM((1, per_device), i32),
            pltpu.VMEM((1, buckets), f32),
            pltpu.VMEM((buckets, buckets), f32),
            pltpu.VMEM((1, cpty_dev), f32),
            pltpu.VMEM((1, msg_lanes), f32),
            pltpu.VMEM((owners, 1, msg_lanes), f32),
            pltpu.VMEM((TERMS, trades, trades), bf16),
            pltpu.VMEM((trades, 8), i32),
            pltpu.VMEM((buckets, trades), bf16),
            pltpu.VMEM((cptys, trades), bf16),
            pltpu.VMEM((path_share, trades), bf16),
            pltpu.VMEM((owners, cpty_dev, path_share), f32),
            pltpu.VMEM((owners, cpty_dev, path_share), f32),
            dma((8,)), dma((pieces,)), dma((pieces,)), dma((pieces,)), dma((pieces,)), dma((pieces,)),
            dma((owners * PIECES,)), dma((owners * PIECES,)),
            dma((owners,)), dma((owners,)), dma((owners,)), dma((owners,)),
            dma((pieces,)), dma((pieces,)), dma((pieces,)), dma((pieces,)), dma((pieces,)),
        ],
        compiler_params=pltpu.CompilerParams(
            collective_id=0, has_side_effects=True, vmem_limit_bytes=40 * 1024 * 1024
        ),
    )(
        basis_values, coefficients, trade_cpty[None, :], trade_bucket[None, :],
        risk_weights[None, :], correlation, funding_spread[None, :],
    )
    return (margin, adj.reshape(path_rows, width))


def margin_terms(arrived, got_codes, risk_weights, correlation, funding_spread):
    path_rows = arrived.shape[0]
    cpty_count = funding_spread.shape[0]
    bucket_count = risk_weights.shape[0]
    is_filled = got_codes >= 0
    column_ids = jnp.arange(cpty_count * bucket_count, dtype=jnp.int32)
    hot_table = (got_codes[:, None] == column_ids[None, :]).astype(jnp.bfloat16)
    bucket_sums = jnp.dot(arrived, hot_table, preferred_element_type=jnp.float32)
    weighted = (
        bucket_sums.reshape(path_rows, cpty_count, bucket_count) * risk_weights[None, None, :]
    )
    rho_w = jnp.einsum("pcb,db->pcd", weighted, correlation, precision=lax.Precision.HIGHEST)
    margin_now = jnp.sqrt(jnp.sum(weighted * rho_w, axis=2) + 1e-06)
    sens_bar = (
        funding_spread[None, :, None] * risk_weights[None, None, :] * rho_w / margin_now[:, :, None]
    )
    flat_bar = sens_bar.reshape(path_rows, cpty_count * bucket_count)
    safe_codes = jnp.where(is_filled, got_codes, 0)
    slot_bar = jnp.take(flat_bar, safe_codes, axis=1) * is_filled[None, :].astype(jnp.float32)
    return (margin_now, slot_bar.astype(jnp.bfloat16))


def body(
    basis_values, coefficients, trade_cpty, trade_bucket, risk_weights, correlation, funding_spread
):
    owners = lax.axis_size("trade")
    per_device = coefficients.shape[0]
    capacity = max(2, 2 * per_device // owners)
    slot_total = owners * capacity
    cpty_count = funding_spread.shape[0]
    bucket_count = risk_weights.shape[0]
    path_rows = basis_values.shape[0]
    owner_of = trade_cpty // cpty_count
    trade_code = trade_cpty % cpty_count * bucket_count + trade_bucket
    position = jnp.arange(per_device, dtype=jnp.int32)
    same_owner = owner_of[:, None] == owner_of[None, :]
    earlier = position[None, :] < position[:, None]
    rank_in = jnp.sum((same_owner & earlier).astype(jnp.int32), axis=1)
    slot_index = owner_of * capacity + rank_in
    codes_out = jnp.full((slot_total,), -1, jnp.int32).at[slot_index].set(trade_code)
    got_codes = lax.all_to_all(codes_out, "trade", split_axis=0, concat_axis=0, tiled=True)
    delta_rows = lax.dot_general(
        basis_values, coefficients, (((1,), (1,)), ((), ())), preferred_element_type=jnp.float32
    ).astype(jnp.bfloat16)
    outgoing = jnp.zeros((path_rows, slot_total), jnp.bfloat16).at[:, slot_index].set(delta_rows)
    arrived = lax.all_to_all(outgoing, "trade", split_axis=1, concat_axis=1, tiled=True)
    margin_now, slot_bar = margin_terms(
        arrived, got_codes, risk_weights, correlation, funding_spread
    )
    returned = lax.all_to_all(slot_bar, "trade", split_axis=1, concat_axis=1, tiled=True)
    delta_bar = returned[:, slot_index]
    partial_adj = jnp.dot(delta_bar, coefficients, preferred_element_type=jnp.float32)
    basis_adjoint = lax.psum(partial_adj, "trade").astype(jnp.bfloat16)
    return (margin_now.T, basis_adjoint)


def solution(mesh):
    placed = (
        P(("date", "path"), None),
        P(("date", "trade"), None),
        P("trade"),
        P("trade"),
        P(),
        P(),
        P("trade"),
    )
    whole = split_paths if mesh.shape["trade"] == 2 * DEEP else body
    return jax.shard_map(
        whole,
        mesh=mesh,
        in_specs=placed,
        out_specs=(P("trade", ("date", "path")), P(("date", "path"), None)),
        check_vma=False,
    )
```

```python
import functools
import jax
import jax.numpy as jnp
from jax import lax
from jax.experimental import pallas as pl
from jax.experimental.pallas import tpu as pltpu
from jax.sharding import PartitionSpec as P

MESH = pl.DeviceIdType.MESH
TERMS = 2
PIECES = 2
DEEP = 4


def split_terms(value, count):
    parts = []
    for _ in range(count):
        head = value.astype(jnp.bfloat16)
        parts.append(head)
        value = value - head.astype(jnp.float32)
    return parts


def dot_nt(a, b):
    return lax.dot_general(a, b, (((1,), (1,)), ((), ())), preferred_element_type=jnp.float32)


def dot_nn(a, b):
    return jnp.dot(a, b, preferred_element_type=jnp.float32)


def margin_kernel(
    owners, basis_in, coef_in, cpty_in, bucket_in, rw_in, corr_in, spread_in,
    adj_ref, margin_ref,
    held, rows_buf, cpty_buf, bucket_buf, rw_buf, corr_buf, spread_buf,
    msg, msgs, gram, cols_buf, bucket_hot, cpty_hot, bar_buf, msend, mrecv,
    local, zu, zd, zr, xs, xr, cs, cr, gs, gr, ms, mr, az_u, az_d, az_r, ax_s, ax_r,
):
    t = lax.axis_index("trade")
    k = lax.axis_index("path")
    z = t // 2
    x = t % 2
    per_device, width = coef_in.shape
    half = per_device // 2
    span = width // PIECES
    buckets = corr_in.shape[0]
    trades = owners * per_device
    path_share = rows_buf.shape[0]
    cpty_dev = mrecv.shape[1]
    cptys = owners * cpty_dev
    code_lanes = -(-per_device // 128) * 128

    def slot(zz, xx, rz, rx):
        return (xx + rx) % 2 * 4 + (zz // 2 + rz // 2) % 2 * 2 + zz % 2

    def send(src, dst, send_sem, recv_sem, to_trade, to_path):
        return pltpu.make_async_remote_copy(
            src_ref=src, dst_ref=dst, send_sem=send_sem, recv_sem=recv_sem,
            device_id={"trade": to_trade, "path": to_path}, device_id_type=MESH,
        )

    own = slot(z, x, z, x)
    small = [
        pltpu.make_async_copy(cpty_in, cpty_buf, local.at[0]),
        pltpu.make_async_copy(bucket_in, bucket_buf, local.at[1]),
        pltpu.make_async_copy(spread_in, spread_buf, local.at[2]),
    ]
    shard = [
        pltpu.make_async_copy(
            coef_in.at[pl.ds(kk * half, half)], held.at[own * 2 + kk], local.at[3 + kk]
        )
        for kk in range(2)
    ]
    rest = [
        pltpu.make_async_copy(rw_in, rw_buf, local.at[5]),
        pltpu.make_async_copy(corr_in, corr_buf, local.at[6]),
        pltpu.make_async_copy(
            basis_in.at[pl.ds(pl.multiple_of(t * path_share, 16), path_share)], rows_buf, local.at[7]
        ),
    ]
    for copy in small + shard + rest:
        copy.start()

    barrier = pltpu.get_barrier_semaphore()
    for step in range(1, owners):
        pl.semaphore_signal(
            barrier, inc=1, device_id={"trade": (t + step) % owners, "path": k}, device_id_type=MESH
        )
    pl.semaphore_signal(barrier, inc=1, device_id={"trade": t, "path": 1 - k}, device_id_type=MESH)

    for copy in small:
        copy.wait()
    msg[...] = jnp.zeros_like(msg)
    msg[:, :per_device] = (cpty_buf[...] * buckets + bucket_buf[...]).astype(jnp.float32)
    msg[:, code_lanes:code_lanes + cpty_dev] = spread_buf[...]
    msgs[0] = msg[...]
    for copy in shard:
        copy.wait()
    pl.semaphore_wait(barrier, owners)

    def msg_copy(step):
        return send(msg, msgs.at[step], gs.at[step], gr.at[step], (t + step) % owners, k)

    def piece(where, p):
        return held.at[where * 2 + k, :, pl.ds(p * span, span)]

    def hop(zz, xx, p, sems, arrive, rz, rx):
        return send(
            piece(slot(zz, xx, z, x), p), piece(slot(zz, xx, rz, rx), p),
            sems.at[zz * PIECES + p], arrive.at[zz * PIECES + p], rz * 2 + rx, k,
        )

    def up(zz, p):
        return hop(zz, x, p, zu, zr, z + 1, x)

    def down(zz, p):
        return hop(zz, x, p, zd, zr, z - 1, x)

    def across(zz, p):
        return hop(zz, x, p, xs, xr, z, 1 - x)

    def over(where, p):
        ref = piece(where, p)
        sem = where * PIECES + p
        return send(ref, ref, cs.at[sem], cr.at[sem], t, 1 - k)

    def chain_arrived(zz, p):
        ref = piece(slot(zz, x, z, x), p)
        sem = zz * PIECES + p
        send(ref, ref, zu.at[sem], zr.at[sem], z * 2 + 1 - x, k).wait_recv()

    def across_arrived(zz, p):
        ref = piece(slot(zz, 1 - x, z, x), p)
        sem = zz * PIECES + p
        send(ref, ref, xs.at[sem], xr.at[sem], z * 2 + 1 - x, k).wait_recv()

    for p in range(PIECES):
        @pl.when(z < DEEP - 1)
        def _():
            up(z, p).start()

        @pl.when(z > 0)
        def _():
            down(z, p).start()

        across(z, p).start()
        if p == 0:
            for step in range(1, owners):
                msg_copy(step).start()

    def chain_arrival(j, p):
        @pl.when(z - j >= 0)
        def _():
            zz = z - j
            chain_arrived(zz, p)

            @pl.when(z < DEEP - 1)
            def _():
                up(zz, p).start()
            across(zz, p).start()
            over(slot(zz, x, z, x), p).start()

        @pl.when(z + j < DEEP)
        def _():
            zz = z + j
            chain_arrived(zz, p)

            @pl.when(z > 0)
            def _():
                down(zz, p).start()
            across(zz, p).start()
            over(slot(zz, x, z, x), p).start()

    def across_at(zz, p):
        across_arrived(zz, p)
        over(slot(zz, 1 - x, z, x), p).start()

    def across_arrival(j, p):
        if j == 0:
            across_at(z, p)
            return

        @pl.when(z - j >= 0)
        def _():
            across_at(z - j, p)

        @pl.when(z + j < DEEP)
        def _():
            across_at(z + j, p)

    for copy in rest:
        copy.wait()
    rw_rows = jnp.broadcast_to(rw_buf[...], (buckets, buckets))
    scaled = corr_buf[...] * rw_rows * rw_rows.T
    scaled_terms = jnp.concatenate(split_terms(scaled, TERMS), axis=1)

    chain_arrival(1, 0)
    for step in range(1, owners):
        msg_copy(step).wait_recv()

    def sender(i):
        zz = (i // 2 + z // 2) % 2 * 2 + i % 2
        return zz * 2 + (i // 4 + x) % 2

    codes = jnp.concatenate(
        [msgs[(t - sender(i)) % owners][:, :per_device] for i in range(owners)], axis=1
    ).astype(jnp.int32)
    spread = jnp.concatenate(
        [msgs[(t - o) % owners][:, code_lanes:code_lanes + cpty_dev] for o in range(owners)], axis=1
    )
    cpty_row = codes // buckets
    bucket_row = codes % buckets
    bucket_hot[...] = (
        lax.broadcasted_iota(jnp.int32, (buckets, trades), 0) == bucket_row
    ).astype(jnp.float32).astype(jnp.bfloat16)
    cpty_hot[...] = (
        lax.broadcasted_iota(jnp.int32, (cptys, trades), 0) == cpty_row
    ).astype(jnp.float32).astype(jnp.bfloat16)
    cols_buf[...] = jnp.broadcast_to(codes.astype(jnp.float32), (8, trades)).T.astype(jnp.int32)

    def build(first, last):
        @pl.loop(first, last)
        def _(i):
            rows = pl.ds(pl.multiple_of(i * per_device, 16), per_device)
            code_col = cols_buf[rows, :1]
            hot = (
                lax.broadcasted_iota(jnp.int32, (per_device, buckets), 1) == code_col % buckets
            ).astype(jnp.float32).astype(jnp.bfloat16)
            same = code_col // buckets == cpty_row
            picked = dot_nn(hot, scaled_terms).astype(jnp.bfloat16)
            stacked = jnp.concatenate(
                [picked[:, term * buckets:(term + 1) * buckets] for term in range(TERMS)], axis=0
            )
            blocks = dot_nn(stacked, bucket_hot[...])
            for term in range(TERMS):
                block = blocks[term * per_device:(term + 1) * per_device]
                gram[term, rows, :] = jnp.where(same, block, 0.0).astype(jnp.bfloat16)

    def deltas(pair):
        for where in (2 * pair, 2 * pair + 1):
            for p in range(PIECES):
                if pair == 0:
                    @pl.when(where != own)
                    def _():
                        over(where, p).wait_recv()
                else:
                    over(where, p).wait_recv()
        rows = slice(pair * 2 * per_device, (pair + 1) * 2 * per_device)
        coef_rows = held[pair * 4:pair * 4 + 4].reshape(2 * per_device, width)
        delta = dot_nt(rows_buf[...], coef_rows).astype(jnp.bfloat16)
        out = dot_nn(delta, gram[TERMS - 1, rows, :])
        for term in range(TERMS - 2, -1, -1):
            out = out + dot_nn(delta, gram[term, rows, :])
        return delta.astype(jnp.float32), out

    across_arrival(0, 0)
    chain_arrival(1, 1)
    across_arrival(0, 1)
    build(0, 1)
    chain_arrival(2, 0)
    build(1, 2)
    chain_arrival(2, 1)
    build(2, 3)
    across_arrival(1, 0)
    chain_arrival(3, 0)
    build(3, 4)
    across_arrival(1, 1)
    chain_arrival(3, 1)
    build(4, 8)
    across_arrival(2, 0)
    across_arrival(2, 1)
    d0, v0 = deltas(0)
    d1, v1 = deltas(1)
    across_arrival(3, 0)
    across_arrival(3, 1)
    d2, v2 = deltas(2)
    early = v0 + v1 + v2
    d3, v3 = deltas(3)
    v = early + v3

    delta_all = jnp.concatenate([d0, d1, d2, d3], axis=1)
    terms = jnp.concatenate(split_terms(delta_all * v, 3), axis=0)
    sums = dot_nt(terms, cpty_hot[...])
    quad = sums[:path_share] + (sums[path_share:2 * path_share] + sums[2 * path_share:])
    margin = jnp.sqrt(quad + 1e-06)
    ratio_terms = jnp.concatenate(split_terms(spread / margin, 3), axis=0)
    spans = dot_nn(ratio_terms, cpty_hot[...])
    ratio = spans[:path_share] + (spans[path_share:2 * path_share] + spans[2 * path_share:])
    bar_buf[...] = (ratio * v).astype(jnp.bfloat16)

    def a_piece(zz, xx, p):
        return adj_ref.at[zz * 2 + xx, :, pl.ds(p * span, span)]

    def a_up(zz, p):
        ref = a_piece(zz, x, p)
        sem = zz * PIECES + p
        return send(ref, ref, az_u.at[sem], az_r.at[sem], (z + 1) * 2 + x, k)

    def a_down(zz, p):
        ref = a_piece(zz, x, p)
        sem = zz * PIECES + p
        return send(ref, ref, az_d.at[sem], az_r.at[sem], (z - 1) * 2 + x, k)

    def a_across(zz, xx, p):
        ref = a_piece(zz, xx, p)
        sem = zz * PIECES + p
        return send(ref, ref, ax_s.at[sem], ax_r.at[sem], z * 2 + 1 - x, k)

    for p in range(PIECES):
        lanes = slice(p * span, (p + 1) * span)
        coef_all = held[:, :, lanes].reshape(trades, span)
        adj_ref[t, :, lanes] = dot_nn(bar_buf[...], coef_all).astype(jnp.bfloat16)

        @pl.when(z < DEEP - 1)
        def _():
            a_up(z, p).start()

        @pl.when(z > 0)
        def _():
            a_down(z, p).start()

        a_across(z, x, p).start()

    flipped = jnp.concatenate([margin, margin], axis=0).T[:, :path_share]
    msend[...] = flipped.reshape(owners, cpty_dev, path_share)

    def margin_copy(step):
        to = (t + step) % owners
        return send(msend.at[to], mrecv.at[step], ms.at[step], mr.at[step], to, k)

    for step in range(1, owners):
        margin_copy(step).start()

    for j in range(1, DEEP):
        for p in range(PIECES):
            @pl.when(z - j >= 0)
            def _():
                a_up(z - j, p).wait_recv()

                @pl.when(z < DEEP - 1)
                def _():
                    a_up(z - j, p).start()
                a_across(z - j, x, p).start()

            @pl.when(z + j < DEEP)
            def _():
                a_down(z + j, p).wait_recv()

                @pl.when(z > 0)
                def _():
                    a_down(z + j, p).start()
                a_across(z + j, x, p).start()

    for step in range(1, owners):
        margin_copy(step).wait_recv()
    mrecv[0] = msend[t]
    for first in range(0, owners, 2):
        pair = [mrecv[(t - o) % owners] for o in (first, first + 1)]
        margin_ref[:, first * path_share:(first + 2) * path_share] = jnp.concatenate(pair, axis=1)

    for zz in range(DEEP):
        for p in range(PIECES):
            a_across(zz, 1 - x, p).wait_recv()

    for step in range(1, owners):
        msg_copy(step).wait_send()
        margin_copy(step).wait_send()
    for p in range(PIECES):
        for where in range(owners):
            @pl.when(where != own)
            def _():
                over(where, p).wait_send()
        for zz in range(DEEP):
            across(zz, p).wait_send()
            a_across(zz, x, p).wait_send()

            @pl.when((zz <= z) & (z < DEEP - 1))
            def _():
                up(zz, p).wait_send()
                a_up(zz, p).wait_send()

            @pl.when((zz >= z) & (z > 0))
            def _():
                down(zz, p).wait_send()
                a_down(zz, p).wait_send()


def split_paths(
    basis_values, coefficients, trade_cpty, trade_bucket, risk_weights, correlation, funding_spread
):
    owners = lax.axis_size("trade")
    per_device, width = coefficients.shape
    cpty_dev = funding_spread.shape[0]
    buckets = risk_weights.shape[0]
    path_rows = basis_values.shape[0]
    path_share = path_rows // owners
    trades = owners * per_device
    cptys = owners * cpty_dev
    vmem = pl.BlockSpec(memory_space=pltpu.VMEM)
    hbm = pl.BlockSpec(memory_space=pltpu.HBM)
    dma = pltpu.SemaphoreType.DMA
    f32, i32, bf16 = jnp.float32, jnp.int32, jnp.bfloat16
    msg_lanes = -(-per_device // 128) * 128 + 128
    pieces = DEEP * PIECES
    adj, margin = pl.pallas_call(
        functools.partial(margin_kernel, owners),
        out_shape=(
            jax.ShapeDtypeStruct((owners, path_share, width), bf16),
            jax.ShapeDtypeStruct((cpty_dev, path_rows), f32),
        ),
        in_specs=[hbm] * 7,
        out_specs=(vmem, vmem),
        scratch_shapes=[
            pltpu.VMEM((owners * 2, per_device // 2, width), bf16),
            pltpu.VMEM((path_share, width), bf16),
            pltpu.VMEM((1, per_device), i32),
            pltpu.VMEM((1, per_device), i32),
            pltpu.VMEM((1, buckets), f32),
            pltpu.VMEM((buckets, buckets), f32),
            pltpu.VMEM((1, cpty_dev), f32),
            pltpu.VMEM((1, msg_lanes), f32),
            pltpu.VMEM((owners, 1, msg_lanes), f32),
            pltpu.VMEM((TERMS, trades, trades), bf16),
            pltpu.VMEM((trades, 8), i32),
            pltpu.VMEM((buckets, trades), bf16),
            pltpu.VMEM((cptys, trades), bf16),
            pltpu.VMEM((path_share, trades), bf16),
            pltpu.VMEM((owners, cpty_dev, path_share), f32),
            pltpu.VMEM((owners, cpty_dev, path_share), f32),
            dma((8,)), dma((pieces,)), dma((pieces,)), dma((pieces,)), dma((pieces,)), dma((pieces,)),
            dma((owners * PIECES,)), dma((owners * PIECES,)),
            dma((owners,)), dma((owners,)), dma((owners,)), dma((owners,)),
            dma((pieces,)), dma((pieces,)), dma((pieces,)), dma((pieces,)), dma((pieces,)),
        ],
        compiler_params=pltpu.CompilerParams(
            collective_id=0, has_side_effects=True, vmem_limit_bytes=56 * 1024 * 1024
        ),
    )(
        basis_values, coefficients, trade_cpty[None, :], trade_bucket[None, :],
        risk_weights[None, :], correlation, funding_spread[None, :],
    )
    return (margin, adj.reshape(path_rows, width))


def margin_terms(arrived, got_codes, risk_weights, correlation, funding_spread):
    path_rows = arrived.shape[0]
    cpty_count = funding_spread.shape[0]
    bucket_count = risk_weights.shape[0]
    is_filled = got_codes >= 0
    column_ids = jnp.arange(cpty_count * bucket_count, dtype=jnp.int32)
    hot_table = (got_codes[:, None] == column_ids[None, :]).astype(jnp.bfloat16)
    bucket_sums = jnp.dot(arrived, hot_table, preferred_element_type=jnp.float32)
    weighted = (
        bucket_sums.reshape(path_rows, cpty_count, bucket_count) * risk_weights[None, None, :]
    )
    rho_w = jnp.einsum("pcb,db->pcd", weighted, correlation, precision=lax.Precision.HIGHEST)
    margin_now = jnp.sqrt(jnp.sum(weighted * rho_w, axis=2) + 1e-06)
    sens_bar = (
        funding_spread[None, :, None] * risk_weights[None, None, :] * rho_w / margin_now[:, :, None]
    )
    flat_bar = sens_bar.reshape(path_rows, cpty_count * bucket_count)
    safe_codes = jnp.where(is_filled, got_codes, 0)
    slot_bar = jnp.take(flat_bar, safe_codes, axis=1) * is_filled[None, :].astype(jnp.float32)
    return (margin_now, slot_bar.astype(jnp.bfloat16))


def body(
    basis_values, coefficients, trade_cpty, trade_bucket, risk_weights, correlation, funding_spread
):
    owners = lax.axis_size("trade")
    per_device = coefficients.shape[0]
    capacity = max(2, 2 * per_device // owners)
    slot_total = owners * capacity
    cpty_count = funding_spread.shape[0]
    bucket_count = risk_weights.shape[0]
    path_rows = basis_values.shape[0]
    owner_of = trade_cpty // cpty_count
    trade_code = trade_cpty % cpty_count * bucket_count + trade_bucket
    position = jnp.arange(per_device, dtype=jnp.int32)
    same_owner = owner_of[:, None] == owner_of[None, :]
    earlier = position[None, :] < position[:, None]
    rank_in = jnp.sum((same_owner & earlier).astype(jnp.int32), axis=1)
    slot_index = owner_of * capacity + rank_in
    codes_out = jnp.full((slot_total,), -1, jnp.int32).at[slot_index].set(trade_code)
    got_codes = lax.all_to_all(codes_out, "trade", split_axis=0, concat_axis=0, tiled=True)
    delta_rows = lax.dot_general(
        basis_values, coefficients, (((1,), (1,)), ((), ())), preferred_element_type=jnp.float32
    ).astype(jnp.bfloat16)
    outgoing = jnp.zeros((path_rows, slot_total), jnp.bfloat16).at[:, slot_index].set(delta_rows)
    arrived = lax.all_to_all(outgoing, "trade", split_axis=1, concat_axis=1, tiled=True)
    margin_now, slot_bar = margin_terms(
        arrived, got_codes, risk_weights, correlation, funding_spread
    )
    returned = lax.all_to_all(slot_bar, "trade", split_axis=1, concat_axis=1, tiled=True)
    delta_bar = returned[:, slot_index]
    partial_adj = jnp.dot(delta_bar, coefficients, preferred_element_type=jnp.float32)
    basis_adjoint = lax.psum(partial_adj, "trade").astype(jnp.bfloat16)
    return (margin_now.T, basis_adjoint)


def solution(mesh):
    placed = (
        P(("date", "path"), None),
        P(("date", "trade"), None),
        P("trade"),
        P("trade"),
        P(),
        P(),
        P("trade"),
    )
    whole = split_paths if mesh.shape["trade"] == 2 * DEEP else body
    return jax.shard_map(
        whole,
        mesh=mesh,
        in_specs=placed,
        out_specs=(P("trade", ("date", "path")), P(("date", "path"), None)),
        check_vma=False,
    )
```

```python
import functools
import jax
import jax.numpy as jnp
from jax import lax
from jax.experimental import pallas as pl
from jax.experimental.pallas import tpu as pltpu
from jax.sharding import PartitionSpec as P

MESH = pl.DeviceIdType.MESH
TERMS = 2
PIECES = 2
ADJ_PIECES = 4
DEEP = 4


def split_terms(value, count):
    parts = []
    for _ in range(count):
        head = value.astype(jnp.bfloat16)
        parts.append(head)
        value = value - head.astype(jnp.float32)
    return parts


def dot_nt(a, b):
    return lax.dot_general(a, b, (((1,), (1,)), ((), ())), preferred_element_type=jnp.float32)


def dot_nn(a, b):
    return jnp.dot(a, b, preferred_element_type=jnp.float32)


def margin_kernel(
    owners, basis_in, coef_in, cpty_in, bucket_in, rw_in, corr_in, spread_in,
    adj_out, margin_out,
    held, adj_ref, margin_ref, rows_buf, cpty_buf, bucket_buf, rw_buf, corr_buf, spread_buf,
    msg, msgs, gram, cols_buf, bucket_hot, cpty_hot, bar_buf, msend, mrecv,
    local, zu, zd, zr, xs, xr, cs, cr, gs, gr, ms, mr, az_u, az_d, az_r, ax_s, ax_r, outs,
):
    t = lax.axis_index("trade")
    k = lax.axis_index("path")
    z = t // 2
    x = t % 2
    per_device, width = coef_in.shape
    half = per_device // 2
    span = width // PIECES
    adj_span = width // ADJ_PIECES
    buckets = corr_in.shape[0]
    trades = owners * per_device
    path_share = rows_buf.shape[0]
    cpty_dev = mrecv.shape[1]
    cptys = owners * cpty_dev
    code_lanes = -(-per_device // 128) * 128

    def slot(zz, xx, rz, rx):
        return (xx + rx) % 2 * 4 + (zz // 2 + rz // 2) % 2 * 2 + zz % 2

    def send(src, dst, send_sem, recv_sem, to_trade, to_path):
        return pltpu.make_async_remote_copy(
            src_ref=src, dst_ref=dst, send_sem=send_sem, recv_sem=recv_sem,
            device_id={"trade": to_trade, "path": to_path}, device_id_type=MESH,
        )

    own = slot(z, x, z, x)
    small = [
        pltpu.make_async_copy(cpty_in, cpty_buf, local.at[0]),
        pltpu.make_async_copy(bucket_in, bucket_buf, local.at[1]),
        pltpu.make_async_copy(spread_in, spread_buf, local.at[2]),
    ]
    shard = [
        pltpu.make_async_copy(
            coef_in.at[pl.ds(kk * half, half)], held.at[own * 2 + kk], local.at[3 + kk]
        )
        for kk in range(2)
    ]
    rest = [
        pltpu.make_async_copy(rw_in, rw_buf, local.at[5]),
        pltpu.make_async_copy(corr_in, corr_buf, local.at[6]),
        pltpu.make_async_copy(
            basis_in.at[pl.ds(pl.multiple_of(t * path_share, 16), path_share)], rows_buf, local.at[7]
        ),
    ]
    for copy in small + shard + rest:
        copy.start()

    barrier = pltpu.get_barrier_semaphore()
    for step in range(1, owners):
        pl.semaphore_signal(
            barrier, inc=1, device_id={"trade": (t + step) % owners, "path": k}, device_id_type=MESH
        )
    pl.semaphore_signal(barrier, inc=1, device_id={"trade": t, "path": 1 - k}, device_id_type=MESH)

    for copy in small:
        copy.wait()
    msg[...] = jnp.zeros_like(msg)
    msg[:, :per_device] = (cpty_buf[...] * buckets + bucket_buf[...]).astype(jnp.float32)
    msg[:, code_lanes:code_lanes + cpty_dev] = spread_buf[...]
    msgs[0] = msg[...]
    for copy in shard:
        copy.wait()
    pl.semaphore_wait(barrier, owners)

    def msg_copy(step):
        return send(msg, msgs.at[step], gs.at[step], gr.at[step], (t + step) % owners, k)

    def piece(where, p):
        return held.at[where * 2 + k, :, pl.ds(p * span, span)]

    def hop(zz, xx, p, sems, arrive, rz, rx):
        return send(
            piece(slot(zz, xx, z, x), p), piece(slot(zz, xx, rz, rx), p),
            sems.at[zz * PIECES + p], arrive.at[zz * PIECES + p], rz * 2 + rx, k,
        )

    def up(zz, p):
        return hop(zz, x, p, zu, zr, z + 1, x)

    def down(zz, p):
        return hop(zz, x, p, zd, zr, z - 1, x)

    def across(zz, p):
        return hop(zz, x, p, xs, xr, z, 1 - x)

    def over(where, p):
        ref = piece(where, p)
        sem = where * PIECES + p
        return send(ref, ref, cs.at[sem], cr.at[sem], t, 1 - k)

    def chain_arrived(zz, p):
        ref = piece(slot(zz, x, z, x), p)
        sem = zz * PIECES + p
        send(ref, ref, zu.at[sem], zr.at[sem], z * 2 + 1 - x, k).wait_recv()

    def across_arrived(zz, p):
        ref = piece(slot(zz, 1 - x, z, x), p)
        sem = zz * PIECES + p
        send(ref, ref, xs.at[sem], xr.at[sem], z * 2 + 1 - x, k).wait_recv()

    for p in range(PIECES):
        @pl.when(z < DEEP - 1)
        def _():
            up(z, p).start()

        @pl.when(z > 0)
        def _():
            down(z, p).start()

        across(z, p).start()
        if p == 0:
            for step in range(1, owners):
                msg_copy(step).start()

    def chain_arrival(j, p):
        @pl.when(z - j >= 0)
        def _():
            zz = z - j
            chain_arrived(zz, p)

            @pl.when(z < DEEP - 1)
            def _():
                up(zz, p).start()
            across(zz, p).start()
            over(slot(zz, x, z, x), p).start()

        @pl.when(z + j < DEEP)
        def _():
            zz = z + j
            chain_arrived(zz, p)

            @pl.when(z > 0)
            def _():
                down(zz, p).start()
            across(zz, p).start()
            over(slot(zz, x, z, x), p).start()

    def across_at(zz, p):
        across_arrived(zz, p)
        over(slot(zz, 1 - x, z, x), p).start()

    def across_arrival(j, p):
        if j == 0:
            across_at(z, p)
            return

        @pl.when(z - j >= 0)
        def _():
            across_at(z - j, p)

        @pl.when(z + j < DEEP)
        def _():
            across_at(z + j, p)

    for copy in rest:
        copy.wait()
    rw_rows = jnp.broadcast_to(rw_buf[...], (buckets, buckets))
    scaled = corr_buf[...] * rw_rows * rw_rows.T
    scaled_terms = jnp.concatenate(split_terms(scaled, TERMS), axis=1)

    chain_arrival(1, 0)
    chain_arrival(1, 1)
    for step in range(1, owners):
        msg_copy(step).wait_recv()

    def sender(i):
        zz = (i // 2 + z // 2) % 2 * 2 + i % 2
        return zz * 2 + (i // 4 + x) % 2

    codes = jnp.concatenate(
        [msgs[(t - sender(i)) % owners][:, :per_device] for i in range(owners)], axis=1
    ).astype(jnp.int32)
    spread = jnp.concatenate(
        [msgs[(t - o) % owners][:, code_lanes:code_lanes + cpty_dev] for o in range(owners)], axis=1
    )
    cpty_row = codes // buckets
    bucket_row = codes % buckets
    bucket_hot[...] = (
        lax.broadcasted_iota(jnp.int32, (buckets, trades), 0) == bucket_row
    ).astype(jnp.float32).astype(jnp.bfloat16)
    cpty_hot[...] = (
        lax.broadcasted_iota(jnp.int32, (cptys, trades), 0) == cpty_row
    ).astype(jnp.float32).astype(jnp.bfloat16)
    cols_buf[...] = jnp.broadcast_to(codes.astype(jnp.float32), (8, trades)).T.astype(jnp.int32)

    def build(first, last):
        @pl.loop(first, last)
        def _(i):
            rows = pl.ds(pl.multiple_of(i * per_device, 16), per_device)
            code_col = cols_buf[rows, :1]
            hot = (
                lax.broadcasted_iota(jnp.int32, (per_device, buckets), 1) == code_col % buckets
            ).astype(jnp.float32).astype(jnp.bfloat16)
            same = code_col // buckets == cpty_row
            picked = dot_nn(hot, scaled_terms).astype(jnp.bfloat16)
            stacked = jnp.concatenate(
                [picked[:, term * buckets:(term + 1) * buckets] for term in range(TERMS)], axis=0
            )
            blocks = dot_nn(stacked, bucket_hot[...])
            for term in range(TERMS):
                block = blocks[term * per_device:(term + 1) * per_device]
                gram[term, rows, :] = jnp.where(same, block, 0.0).astype(jnp.bfloat16)

    def deltas(first, last):
        for where in range(2 * first, 2 * last):
            for p in range(PIECES):
                if where < 2:
                    @pl.when(where != own)
                    def _():
                        over(where, p).wait_recv()
                else:
                    over(where, p).wait_recv()
        rows = slice(first * 2 * per_device, last * 2 * per_device)
        coef_rows = held[first * 4:last * 4].reshape((last - first) * 2 * per_device, width)
        delta = dot_nt(rows_buf[...], coef_rows).astype(jnp.bfloat16)
        out = dot_nn(delta, gram[TERMS - 1, rows, :])
        for term in range(TERMS - 2, -1, -1):
            out = out + dot_nn(delta, gram[term, rows, :])
        return delta.astype(jnp.float32), out

    chain_arrival(2, 0)
    across_arrival(0, 0)
    across_arrival(0, 1)
    build(0, 1)
    chain_arrival(2, 1)
    build(1, 2)
    chain_arrival(3, 0)
    build(2, 3)
    chain_arrival(3, 1)
    across_arrival(1, 0)
    build(3, 4)
    across_arrival(1, 1)
    build(4, 6)
    across_arrival(2, 0)
    build(6, 8)
    across_arrival(2, 1)
    d0, v0 = deltas(0, 2)
    across_arrival(3, 0)
    across_arrival(3, 1)
    d2, v2 = deltas(2, 3)
    early = v0 + v2
    d3, v3 = deltas(3, 4)
    v = early + v3

    delta_all = jnp.concatenate([d0, d2, d3], axis=1)
    terms = jnp.concatenate(split_terms(delta_all * v, 3), axis=0)
    sums = dot_nt(terms, cpty_hot[...])
    quad = sums[:path_share] + (sums[path_share:2 * path_share] + sums[2 * path_share:])
    margin = jnp.sqrt(quad + 1e-06)
    ratio_terms = jnp.concatenate(split_terms(spread / margin, 3), axis=0)
    spans = dot_nn(ratio_terms, cpty_hot[...])
    ratio = spans[:path_share] + (spans[path_share:2 * path_share] + spans[2 * path_share:])
    bar_buf[...] = (ratio * v).astype(jnp.bfloat16)

    def a_piece(zz, xx, p):
        return adj_ref.at[zz * 2 + xx, :, pl.ds(p * adj_span, adj_span)]

    def a_up(zz, p):
        ref = a_piece(zz, x, p)
        sem = zz * ADJ_PIECES + p
        return send(ref, ref, az_u.at[sem], az_r.at[sem], (z + 1) * 2 + x, k)

    def a_down(zz, p):
        ref = a_piece(zz, x, p)
        sem = zz * ADJ_PIECES + p
        return send(ref, ref, az_d.at[sem], az_r.at[sem], (z - 1) * 2 + x, k)

    def a_across(zz, xx, p):
        ref = a_piece(zz, xx, p)
        sem = zz * ADJ_PIECES + p
        return send(ref, ref, ax_s.at[sem], ax_r.at[sem], z * 2 + 1 - x, k)

    def out_copy(where):
        return pltpu.make_async_copy(adj_ref.at[where], adj_out.at[where], outs.at[where])

    for p in range(ADJ_PIECES):
        if p % (ADJ_PIECES // PIECES) == 0:
            wide = slice(p * adj_span, p * adj_span + span)
            coef_all = held[:, :, wide].reshape(trades, span)
            adj_ref[t, :, wide] = dot_nn(bar_buf[...], coef_all).astype(jnp.bfloat16)

        @pl.when(z < DEEP - 1)
        def _():
            a_up(z, p).start()

        @pl.when(z > 0)
        def _():
            a_down(z, p).start()

        a_across(z, x, p).start()
    out_copy(t).start()

    flipped = jnp.concatenate([margin, margin], axis=0).T[:, :path_share]
    msend[...] = flipped.reshape(owners, cpty_dev, path_share)

    def margin_copy(step):
        to = (t + step) % owners
        return send(msend.at[to], mrecv.at[step], ms.at[step], mr.at[step], to, k)

    for step in range(1, owners):
        margin_copy(step).start()

    for j in range(1, DEEP):
        for p in range(ADJ_PIECES):
            @pl.when(z - j >= 0)
            def _():
                a_up(z - j, p).wait_recv()

                @pl.when(z < DEEP - 1)
                def _():
                    a_up(z - j, p).start()
                a_across(z - j, x, p).start()

            @pl.when(z + j < DEEP)
            def _():
                a_down(z + j, p).wait_recv()

                @pl.when(z > 0)
                def _():
                    a_down(z + j, p).start()
                a_across(z + j, x, p).start()

        @pl.when(z - j >= 0)
        def _():
            out_copy((z - j) * 2 + x).start()

        @pl.when(z + j < DEEP)
        def _():
            out_copy((z + j) * 2 + x).start()

    for step in range(1, owners):
        margin_copy(step).wait_recv()
    mrecv[0] = msend[t]
    for first in range(0, owners, 2):
        pair = [mrecv[(t - o) % owners] for o in (first, first + 1)]
        margin_ref[:, first * path_share:(first + 2) * path_share] = jnp.concatenate(pair, axis=1)
    margin_done = pltpu.make_async_copy(margin_ref, margin_out, local.at[0])
    margin_done.start()

    def adj_across(zz):
        for p in range(ADJ_PIECES):
            a_across(zz, 1 - x, p).wait_recv()
        out_copy(zz * 2 + 1 - x).start()

    adj_across(z)
    for j in range(1, DEEP):
        @pl.when(z - j >= 0)
        def _():
            adj_across(z - j)

        @pl.when(z + j < DEEP)
        def _():
            adj_across(z + j)

    for step in range(1, owners):
        msg_copy(step).wait_send()
        margin_copy(step).wait_send()
    for p in range(PIECES):
        for where in range(owners):
            @pl.when(where != own)
            def _():
                over(where, p).wait_send()
        for zz in range(DEEP):
            across(zz, p).wait_send()

            @pl.when((zz <= z) & (z < DEEP - 1))
            def _():
                up(zz, p).wait_send()

            @pl.when((zz >= z) & (z > 0))
            def _():
                down(zz, p).wait_send()
    for p in range(ADJ_PIECES):
        for zz in range(DEEP):
            a_across(zz, x, p).wait_send()

            @pl.when((zz <= z) & (z < DEEP - 1))
            def _():
                a_up(zz, p).wait_send()

            @pl.when((zz >= z) & (z > 0))
            def _():
                a_down(zz, p).wait_send()
    margin_done.wait()
    for where in range(owners):
        out_copy(where).wait()


def hand_over(adj_in, margin_in, adj_out, margin_out, sems):
    count = adj_in.shape[0]
    copies = [
        pltpu.make_async_copy(adj_in.at[i], adj_out.at[i], sems.at[i]) for i in range(count)
    ]
    copies.append(pltpu.make_async_copy(margin_in, margin_out, sems.at[count]))
    for copy in copies:
        copy.start()
    for copy in copies:
        copy.wait()


def split_paths(
    basis_values, coefficients, trade_cpty, trade_bucket, risk_weights, correlation, funding_spread
):
    owners = lax.axis_size("trade")
    per_device, width = coefficients.shape
    cpty_dev = funding_spread.shape[0]
    buckets = risk_weights.shape[0]
    path_rows = basis_values.shape[0]
    path_share = path_rows // owners
    trades = owners * per_device
    cptys = owners * cpty_dev
    hbm = pl.BlockSpec(memory_space=pltpu.HBM)
    dma = pltpu.SemaphoreType.DMA
    f32, i32, bf16 = jnp.float32, jnp.int32, jnp.bfloat16
    msg_lanes = -(-per_device // 128) * 128 + 128
    pieces = DEEP * PIECES
    adj_pieces = DEEP * ADJ_PIECES
    adj, margin = pl.pallas_call(
        functools.partial(margin_kernel, owners),
        out_shape=(
            jax.ShapeDtypeStruct((owners, path_share, width), bf16),
            jax.ShapeDtypeStruct((cpty_dev, path_rows), f32),
        ),
        in_specs=[hbm] * 7,
        out_specs=(hbm, hbm),
        scratch_shapes=[
            pltpu.VMEM((owners * 2, per_device // 2, width), bf16),
            pltpu.VMEM((owners, path_share, width), bf16),
            pltpu.VMEM((cpty_dev, path_rows), f32),
            pltpu.VMEM((path_share, width), bf16),
            pltpu.VMEM((1, per_device), i32),
            pltpu.VMEM((1, per_device), i32),
            pltpu.VMEM((1, buckets), f32),
            pltpu.VMEM((buckets, buckets), f32),
            pltpu.VMEM((1, cpty_dev), f32),
            pltpu.VMEM((1, msg_lanes), f32),
            pltpu.VMEM((owners, 1, msg_lanes), f32),
            pltpu.VMEM((TERMS, trades, trades), bf16),
            pltpu.VMEM((trades, 8), i32),
            pltpu.VMEM((buckets, trades), bf16),
            pltpu.VMEM((cptys, trades), bf16),
            pltpu.VMEM((path_share, trades), bf16),
            pltpu.VMEM((owners, cpty_dev, path_share), f32),
            pltpu.VMEM((owners, cpty_dev, path_share), f32),
            dma((8,)), dma((pieces,)), dma((pieces,)), dma((pieces,)), dma((pieces,)), dma((pieces,)),
            dma((owners * PIECES,)), dma((owners * PIECES,)),
            dma((owners,)), dma((owners,)), dma((owners,)), dma((owners,)),
            dma((adj_pieces,)), dma((adj_pieces,)), dma((adj_pieces,)), dma((adj_pieces,)),
            dma((adj_pieces,)), dma((owners,)),
        ],
        compiler_params=pltpu.CompilerParams(
            collective_id=0, has_side_effects=True, vmem_limit_bytes=56 * 1024 * 1024
        ),
    )(
        basis_values, coefficients, trade_cpty[None, :], trade_bucket[None, :],
        risk_weights[None, :], correlation, funding_spread[None, :],
    )
    adj, margin = pl.pallas_call(
        hand_over,
        out_shape=(
            jax.ShapeDtypeStruct(adj.shape, bf16), jax.ShapeDtypeStruct(margin.shape, f32),
        ),
        in_specs=[hbm, hbm],
        out_specs=(hbm, hbm),
        scratch_shapes=[dma((owners + 1,))],
        compiler_params=pltpu.CompilerParams(vmem_limit_bytes=56 * 1024 * 1024),
    )(adj, margin)
    return (margin, adj.reshape(path_rows, width))


def margin_terms(arrived, got_codes, risk_weights, correlation, funding_spread):
    path_rows = arrived.shape[0]
    cpty_count = funding_spread.shape[0]
    bucket_count = risk_weights.shape[0]
    is_filled = got_codes >= 0
    column_ids = jnp.arange(cpty_count * bucket_count, dtype=jnp.int32)
    hot_table = (got_codes[:, None] == column_ids[None, :]).astype(jnp.bfloat16)
    bucket_sums = jnp.dot(arrived, hot_table, preferred_element_type=jnp.float32)
    weighted = (
        bucket_sums.reshape(path_rows, cpty_count, bucket_count) * risk_weights[None, None, :]
    )
    rho_w = jnp.einsum("pcb,db->pcd", weighted, correlation, precision=lax.Precision.HIGHEST)
    margin_now = jnp.sqrt(jnp.sum(weighted * rho_w, axis=2) + 1e-06)
    sens_bar = (
        funding_spread[None, :, None] * risk_weights[None, None, :] * rho_w / margin_now[:, :, None]
    )
    flat_bar = sens_bar.reshape(path_rows, cpty_count * bucket_count)
    safe_codes = jnp.where(is_filled, got_codes, 0)
    slot_bar = jnp.take(flat_bar, safe_codes, axis=1) * is_filled[None, :].astype(jnp.float32)
    return (margin_now, slot_bar.astype(jnp.bfloat16))


def body(
    basis_values, coefficients, trade_cpty, trade_bucket, risk_weights, correlation, funding_spread
):
    owners = lax.axis_size("trade")
    per_device = coefficients.shape[0]
    capacity = max(2, 2 * per_device // owners)
    slot_total = owners * capacity
    cpty_count = funding_spread.shape[0]
    bucket_count = risk_weights.shape[0]
    path_rows = basis_values.shape[0]
    owner_of = trade_cpty // cpty_count
    trade_code = trade_cpty % cpty_count * bucket_count + trade_bucket
    position = jnp.arange(per_device, dtype=jnp.int32)
    same_owner = owner_of[:, None] == owner_of[None, :]
    earlier = position[None, :] < position[:, None]
    rank_in = jnp.sum((same_owner & earlier).astype(jnp.int32), axis=1)
    slot_index = owner_of * capacity + rank_in
    codes_out = jnp.full((slot_total,), -1, jnp.int32).at[slot_index].set(trade_code)
    got_codes = lax.all_to_all(codes_out, "trade", split_axis=0, concat_axis=0, tiled=True)
    delta_rows = lax.dot_general(
        basis_values, coefficients, (((1,), (1,)), ((), ())), preferred_element_type=jnp.float32
    ).astype(jnp.bfloat16)
    outgoing = jnp.zeros((path_rows, slot_total), jnp.bfloat16).at[:, slot_index].set(delta_rows)
    arrived = lax.all_to_all(outgoing, "trade", split_axis=1, concat_axis=1, tiled=True)
    margin_now, slot_bar = margin_terms(
        arrived, got_codes, risk_weights, correlation, funding_spread
    )
    returned = lax.all_to_all(slot_bar, "trade", split_axis=1, concat_axis=1, tiled=True)
    delta_bar = returned[:, slot_index]
    partial_adj = jnp.dot(delta_bar, coefficients, preferred_element_type=jnp.float32)
    basis_adjoint = lax.psum(partial_adj, "trade").astype(jnp.bfloat16)
    return (margin_now.T, basis_adjoint)


def solution(mesh):
    placed = (
        P(("date", "path"), None),
        P(("date", "trade"), None),
        P("trade"),
        P("trade"),
        P(),
        P(),
        P("trade"),
    )
    whole = split_paths if mesh.shape["trade"] == 2 * DEEP else body
    return jax.shard_map(
        whole,
        mesh=mesh,
        in_specs=placed,
        out_specs=(P("trade", ("date", "path")), P(("date", "path"), None)),
        check_vma=False,
    )
```

```python
import functools
import jax
import jax.numpy as jnp
from jax import lax
from jax.experimental import pallas as pl
from jax.experimental.pallas import tpu as pltpu
from jax.sharding import PartitionSpec as P

MESH = pl.DeviceIdType.MESH
TERMS = 2
PIECES = 2
ADJ_PIECES = 4
DEEP = 4


def split_terms(value, count):
    parts = []
    for _ in range(count):
        head = value.astype(jnp.bfloat16)
        parts.append(head)
        value = value - head.astype(jnp.float32)
    return parts


def dot_nt(a, b):
    return lax.dot_general(a, b, (((1,), (1,)), ((), ())), preferred_element_type=jnp.float32)


def dot_nn(a, b):
    return jnp.dot(a, b, preferred_element_type=jnp.float32)


def margin_kernel(
    owners, basis_in, coef_in, cpty_in, bucket_in, rw_in, corr_in, spread_in,
    adj_out, margin_out,
    held, adj_ref, margin_ref, rows_buf, cpty_buf, bucket_buf, rw_buf, corr_buf, spread_buf,
    msg, msgs, gram, cols_buf, bucket_hot, cpty_hot, cpty_cols, bar_buf, msend, mrecv,
    local, zu, zd, zr, xs, xr, cs, cr, gs, gr, ms, mr, az_u, az_d, az_r, ax_s, ax_r, outs,
):
    t = lax.axis_index("trade")
    k = lax.axis_index("path")
    z = t // 2
    x = t % 2
    per_device, width = coef_in.shape
    half = per_device // 2
    span = width // PIECES
    adj_span = width // ADJ_PIECES
    buckets = corr_in.shape[0]
    trades = owners * per_device
    path_share = rows_buf.shape[0]
    cpty_dev = mrecv.shape[1]
    cptys = owners * cpty_dev
    code_lanes = -(-per_device // 128) * 128

    def slot(zz, xx, rz, rx):
        return (xx + rx) % 2 * 4 + (zz // 2 + rz // 2) % 2 * 2 + zz % 2

    def send(src, dst, send_sem, recv_sem, to_trade, to_path):
        return pltpu.make_async_remote_copy(
            src_ref=src, dst_ref=dst, send_sem=send_sem, recv_sem=recv_sem,
            device_id={"trade": to_trade, "path": to_path}, device_id_type=MESH,
        )

    own = slot(z, x, z, x)
    small = [
        pltpu.make_async_copy(cpty_in, cpty_buf, local.at[0]),
        pltpu.make_async_copy(bucket_in, bucket_buf, local.at[1]),
        pltpu.make_async_copy(spread_in, spread_buf, local.at[2]),
    ]
    shard = [
        pltpu.make_async_copy(
            coef_in.at[pl.ds(kk * half, half)], held.at[own * 2 + kk], local.at[3 + kk]
        )
        for kk in range(2)
    ]
    rest = [
        pltpu.make_async_copy(rw_in, rw_buf, local.at[5]),
        pltpu.make_async_copy(corr_in, corr_buf, local.at[6]),
        pltpu.make_async_copy(
            basis_in.at[pl.ds(pl.multiple_of(t * path_share, 16), path_share)], rows_buf, local.at[7]
        ),
    ]
    for copy in small + shard + rest:
        copy.start()

    barrier = pltpu.get_barrier_semaphore()
    for step in range(1, owners):
        pl.semaphore_signal(
            barrier, inc=1, device_id={"trade": (t + step) % owners, "path": k}, device_id_type=MESH
        )
    pl.semaphore_signal(barrier, inc=1, device_id={"trade": t, "path": 1 - k}, device_id_type=MESH)

    for copy in small:
        copy.wait()
    msg[...] = jnp.zeros_like(msg)
    msg[:, :per_device] = (cpty_buf[...] * buckets + bucket_buf[...]).astype(jnp.float32)
    msg[:, code_lanes:code_lanes + cpty_dev] = spread_buf[...]
    msgs[0] = msg[...]
    for copy in shard:
        copy.wait()
    pl.semaphore_wait(barrier, owners)

    def msg_copy(step):
        return send(msg, msgs.at[step], gs.at[step], gr.at[step], (t + step) % owners, k)

    def piece(where, p):
        return held.at[where * 2 + k, :, pl.ds(p * span, span)]

    def hop(zz, xx, p, sems, arrive, rz, rx):
        return send(
            piece(slot(zz, xx, z, x), p), piece(slot(zz, xx, rz, rx), p),
            sems.at[zz * PIECES + p], arrive.at[zz * PIECES + p], rz * 2 + rx, k,
        )

    def up(zz, p):
        return hop(zz, x, p, zu, zr, z + 1, x)

    def down(zz, p):
        return hop(zz, x, p, zd, zr, z - 1, x)

    def across(zz, p):
        return hop(zz, x, p, xs, xr, z, 1 - x)

    def over(where, p):
        ref = piece(where, p)
        sem = where * PIECES + p
        return send(ref, ref, cs.at[sem], cr.at[sem], t, 1 - k)

    def chain_arrived(zz, p):
        ref = piece(slot(zz, x, z, x), p)
        sem = zz * PIECES + p
        send(ref, ref, zu.at[sem], zr.at[sem], z * 2 + 1 - x, k).wait_recv()

    def across_arrived(zz, p):
        ref = piece(slot(zz, 1 - x, z, x), p)
        sem = zz * PIECES + p
        send(ref, ref, xs.at[sem], xr.at[sem], z * 2 + 1 - x, k).wait_recv()

    for p in range(PIECES):
        @pl.when(z < DEEP - 1)
        def _():
            up(z, p).start()

        @pl.when(z > 0)
        def _():
            down(z, p).start()

        across(z, p).start()
        if p == 0:
            for step in range(1, owners):
                msg_copy(step).start()

    def chain_arrival(j, p):
        @pl.when(z - j >= 0)
        def _():
            zz = z - j
            chain_arrived(zz, p)

            @pl.when(z < DEEP - 1)
            def _():
                up(zz, p).start()
            across(zz, p).start()
            over(slot(zz, x, z, x), p).start()

        @pl.when(z + j < DEEP)
        def _():
            zz = z + j
            chain_arrived(zz, p)

            @pl.when(z > 0)
            def _():
                down(zz, p).start()
            across(zz, p).start()
            over(slot(zz, x, z, x), p).start()

    def across_at(zz, p):
        across_arrived(zz, p)
        over(slot(zz, 1 - x, z, x), p).start()

    def across_arrival(j, p):
        if j == 0:
            across_at(z, p)
            return

        @pl.when(z - j >= 0)
        def _():
            across_at(z - j, p)

        @pl.when(z + j < DEEP)
        def _():
            across_at(z + j, p)

    for copy in rest:
        copy.wait()
    rw_rows = jnp.broadcast_to(rw_buf[...], (buckets, buckets))
    scaled = corr_buf[...] * rw_rows * rw_rows.T
    scaled_terms = jnp.concatenate(split_terms(scaled, TERMS), axis=1)

    chain_arrival(1, 0)
    chain_arrival(1, 1)
    for step in range(1, owners):
        msg_copy(step).wait_recv()

    def sender(i):
        zz = (i // 2 + z // 2) % 2 * 2 + i % 2
        return zz * 2 + (i // 4 + x) % 2

    codes = jnp.concatenate(
        [msgs[(t - sender(i)) % owners][:, :per_device] for i in range(owners)], axis=1
    ).astype(jnp.int32)
    spread = jnp.concatenate(
        [msgs[(t - o) % owners][:, code_lanes:code_lanes + cpty_dev] for o in range(owners)], axis=1
    )
    cpty_row = codes // buckets
    bucket_row = codes % buckets
    bucket_hot[...] = (
        lax.broadcasted_iota(jnp.int32, (buckets, trades), 0) == bucket_row
    ).astype(jnp.float32).astype(jnp.bfloat16)
    cpty_hot[...] = (
        lax.broadcasted_iota(jnp.int32, (cptys, trades), 0) == cpty_row
    ).astype(jnp.float32).astype(jnp.bfloat16)
    cols_buf[...] = jnp.broadcast_to(codes.astype(jnp.float32), (8, trades)).T.astype(jnp.int32)

    def build(first, last):
        @pl.loop(first, last)
        def _(i):
            rows = pl.ds(pl.multiple_of(i * per_device, 16), per_device)
            code_col = cols_buf[rows, :1]
            hot = (
                lax.broadcasted_iota(jnp.int32, (per_device, buckets), 1) == code_col % buckets
            ).astype(jnp.float32).astype(jnp.bfloat16)
            same = code_col // buckets == cpty_row
            cpty_cols[rows, :] = (
                lax.broadcasted_iota(jnp.int32, (per_device, cptys), 1) == code_col // buckets
            ).astype(jnp.float32).astype(jnp.bfloat16)
            picked = dot_nn(hot, scaled_terms).astype(jnp.bfloat16)
            stacked = jnp.concatenate(
                [picked[:, term * buckets:(term + 1) * buckets] for term in range(TERMS)], axis=0
            )
            blocks = dot_nn(stacked, bucket_hot[...])
            for term in range(TERMS):
                block = blocks[term * per_device:(term + 1) * per_device]
                gram[term, rows, :] = jnp.where(same, block, 0.0).astype(jnp.bfloat16)

    def deltas(first, last):
        for where in range(2 * first, 2 * last):
            for p in range(PIECES):
                if where < 2:
                    @pl.when(where != own)
                    def _():
                        over(where, p).wait_recv()
                else:
                    over(where, p).wait_recv()
        rows = slice(first * 2 * per_device, last * 2 * per_device)
        coef_rows = held[first * 4:last * 4].reshape((last - first) * 2 * per_device, width)
        delta = dot_nt(rows_buf[...], coef_rows).astype(jnp.bfloat16)
        out = dot_nn(delta, gram[TERMS - 1, rows, :])
        for term in range(TERMS - 2, -1, -1):
            out = out + dot_nn(delta, gram[term, rows, :])
        return delta.astype(jnp.float32), out

    chain_arrival(2, 0)
    across_arrival(0, 0)
    across_arrival(0, 1)
    build(0, 1)
    chain_arrival(2, 1)
    build(1, 2)
    chain_arrival(3, 0)
    build(2, 3)
    chain_arrival(3, 1)
    across_arrival(1, 0)
    build(3, 4)
    across_arrival(1, 1)
    build(4, 6)
    across_arrival(2, 0)
    build(6, 8)
    across_arrival(2, 1)
    d0, v0 = deltas(0, 2)
    across_arrival(3, 0)
    across_arrival(3, 1)
    d2, v2 = deltas(2, 3)
    early = v0 + v2
    d3, v3 = deltas(3, 4)
    v = early + v3

    delta_all = jnp.concatenate([d0, d2, d3], axis=1)
    terms = jnp.concatenate(split_terms(delta_all * v, 3), axis=0)
    sums = dot_nn(terms, cpty_cols[...])
    quad = sums[:path_share] + (sums[path_share:2 * path_share] + sums[2 * path_share:])
    margin = jnp.sqrt(quad + 1e-06)
    ratio_terms = jnp.concatenate(split_terms(spread / margin, 3), axis=0)
    spans = dot_nn(ratio_terms, cpty_hot[...])
    ratio = spans[:path_share] + (spans[path_share:2 * path_share] + spans[2 * path_share:])
    bar_buf[...] = (ratio * v).astype(jnp.bfloat16)

    def a_piece(zz, xx, p):
        return adj_ref.at[zz * 2 + xx, :, pl.ds(p * adj_span, adj_span)]

    def a_up(zz, p):
        ref = a_piece(zz, x, p)
        sem = zz * ADJ_PIECES + p
        return send(ref, ref, az_u.at[sem], az_r.at[sem], (z + 1) * 2 + x, k)

    def a_down(zz, p):
        ref = a_piece(zz, x, p)
        sem = zz * ADJ_PIECES + p
        return send(ref, ref, az_d.at[sem], az_r.at[sem], (z - 1) * 2 + x, k)

    def a_across(zz, xx, p):
        ref = a_piece(zz, xx, p)
        sem = zz * ADJ_PIECES + p
        return send(ref, ref, ax_s.at[sem], ax_r.at[sem], z * 2 + 1 - x, k)

    def out_copy(where):
        return pltpu.make_async_copy(adj_ref.at[where], adj_out.at[where], outs.at[where])

    for p in range(ADJ_PIECES):
        if p % (ADJ_PIECES // PIECES) == 0:
            wide = slice(p * adj_span, p * adj_span + span)
            coef_all = held[:, :, wide].reshape(trades, span)
            adj_ref[t, :, wide] = dot_nn(bar_buf[...], coef_all).astype(jnp.bfloat16)

        @pl.when(z < DEEP - 1)
        def _():
            a_up(z, p).start()

        @pl.when(z > 0)
        def _():
            a_down(z, p).start()

        a_across(z, x, p).start()
    out_copy(t).start()

    flipped = jnp.concatenate([margin, margin], axis=0).T[:, :path_share]
    msend[...] = flipped.reshape(owners, cpty_dev, path_share)

    def margin_copy(step):
        to = (t + step) % owners
        return send(msend.at[to], mrecv.at[step], ms.at[step], mr.at[step], to, k)

    for step in range(1, owners):
        margin_copy(step).start()

    for j in range(1, DEEP):
        for p in range(ADJ_PIECES):
            @pl.when(z - j >= 0)
            def _():
                a_up(z - j, p).wait_recv()

                @pl.when(z < DEEP - 1)
                def _():
                    a_up(z - j, p).start()
                a_across(z - j, x, p).start()

            @pl.when(z + j < DEEP)
            def _():
                a_down(z + j, p).wait_recv()

                @pl.when(z > 0)
                def _():
                    a_down(z + j, p).start()
                a_across(z + j, x, p).start()

        @pl.when(z - j >= 0)
        def _():
            out_copy((z - j) * 2 + x).start()

        @pl.when(z + j < DEEP)
        def _():
            out_copy((z + j) * 2 + x).start()

    for step in range(1, owners):
        margin_copy(step).wait_recv()
    mrecv[0] = msend[t]
    for first in range(0, owners, 2):
        pair = [mrecv[(t - o) % owners] for o in (first, first + 1)]
        margin_ref[:, first * path_share:(first + 2) * path_share] = jnp.concatenate(pair, axis=1)
    margin_done = pltpu.make_async_copy(margin_ref, margin_out, local.at[0])
    margin_done.start()

    def adj_across(zz):
        for p in range(ADJ_PIECES):
            a_across(zz, 1 - x, p).wait_recv()
        out_copy(zz * 2 + 1 - x).start()

    adj_across(z)
    for j in range(1, DEEP):
        @pl.when(z - j >= 0)
        def _():
            adj_across(z - j)

        @pl.when(z + j < DEEP)
        def _():
            adj_across(z + j)

    for step in range(1, owners):
        msg_copy(step).wait_send()
        margin_copy(step).wait_send()
    for p in range(PIECES):
        for where in range(owners):
            @pl.when(where != own)
            def _():
                over(where, p).wait_send()
        for zz in range(DEEP):
            across(zz, p).wait_send()

            @pl.when((zz <= z) & (z < DEEP - 1))
            def _():
                up(zz, p).wait_send()

            @pl.when((zz >= z) & (z > 0))
            def _():
                down(zz, p).wait_send()
    for p in range(ADJ_PIECES):
        for zz in range(DEEP):
            a_across(zz, x, p).wait_send()

            @pl.when((zz <= z) & (z < DEEP - 1))
            def _():
                a_up(zz, p).wait_send()

            @pl.when((zz >= z) & (z > 0))
            def _():
                a_down(zz, p).wait_send()
    margin_done.wait()
    for where in range(owners):
        out_copy(where).wait()


def hand_over(adj_in, margin_in, adj_out, margin_out, adj_held, margin_held, sems):
    count = adj_in.shape[0]
    legs = [(adj_in.at[i], adj_held.at[i], adj_out.at[i]) for i in range(count)]
    legs.append((margin_in, margin_held, margin_out))
    reads = [pltpu.make_async_copy(a, b, sems.at[i]) for i, (a, b, _) in enumerate(legs)]
    writes = [
        pltpu.make_async_copy(b, c, sems.at[count + 1 + i]) for i, (_, b, c) in enumerate(legs)
    ]
    for copy in reads:
        copy.start()
    for read, write in zip(reads, writes):
        read.wait()
        write.start()
    for copy in writes:
        copy.wait()


def split_paths(
    basis_values, coefficients, trade_cpty, trade_bucket, risk_weights, correlation, funding_spread
):
    owners = lax.axis_size("trade")
    per_device, width = coefficients.shape
    cpty_dev = funding_spread.shape[0]
    buckets = risk_weights.shape[0]
    path_rows = basis_values.shape[0]
    path_share = path_rows // owners
    trades = owners * per_device
    cptys = owners * cpty_dev
    hbm = pl.BlockSpec(memory_space=pltpu.HBM)
    dma = pltpu.SemaphoreType.DMA
    f32, i32, bf16 = jnp.float32, jnp.int32, jnp.bfloat16
    msg_lanes = -(-per_device // 128) * 128 + 128
    pieces = DEEP * PIECES
    adj_pieces = DEEP * ADJ_PIECES
    adj, margin = pl.pallas_call(
        functools.partial(margin_kernel, owners),
        out_shape=(
            jax.ShapeDtypeStruct((owners, path_share, width), bf16),
            jax.ShapeDtypeStruct((cpty_dev, path_rows), f32),
        ),
        in_specs=[hbm] * 7,
        out_specs=(hbm, hbm),
        scratch_shapes=[
            pltpu.VMEM((owners * 2, per_device // 2, width), bf16),
            pltpu.VMEM((owners, path_share, width), bf16),
            pltpu.VMEM((cpty_dev, path_rows), f32),
            pltpu.VMEM((path_share, width), bf16),
            pltpu.VMEM((1, per_device), i32),
            pltpu.VMEM((1, per_device), i32),
            pltpu.VMEM((1, buckets), f32),
            pltpu.VMEM((buckets, buckets), f32),
            pltpu.VMEM((1, cpty_dev), f32),
            pltpu.VMEM((1, msg_lanes), f32),
            pltpu.VMEM((owners, 1, msg_lanes), f32),
            pltpu.VMEM((TERMS, trades, trades), bf16),
            pltpu.VMEM((trades, 8), i32),
            pltpu.VMEM((buckets, trades), bf16),
            pltpu.VMEM((cptys, trades), bf16),
            pltpu.VMEM((trades, cptys), bf16),
            pltpu.VMEM((path_share, trades), bf16),
            pltpu.VMEM((owners, cpty_dev, path_share), f32),
            pltpu.VMEM((owners, cpty_dev, path_share), f32),
            dma((8,)), dma((pieces,)), dma((pieces,)), dma((pieces,)), dma((pieces,)), dma((pieces,)),
            dma((owners * PIECES,)), dma((owners * PIECES,)),
            dma((owners,)), dma((owners,)), dma((owners,)), dma((owners,)),
            dma((adj_pieces,)), dma((adj_pieces,)), dma((adj_pieces,)), dma((adj_pieces,)),
            dma((adj_pieces,)), dma((owners,)),
        ],
        compiler_params=pltpu.CompilerParams(
            collective_id=0, has_side_effects=True, vmem_limit_bytes=56 * 1024 * 1024
        ),
    )(
        basis_values, coefficients, trade_cpty[None, :], trade_bucket[None, :],
        risk_weights[None, :], correlation, funding_spread[None, :],
    )
    adj, margin = pl.pallas_call(
        hand_over,
        out_shape=(
            jax.ShapeDtypeStruct(adj.shape, bf16), jax.ShapeDtypeStruct(margin.shape, f32),
        ),
        in_specs=[hbm, hbm],
        out_specs=(hbm, hbm),
        scratch_shapes=[
            pltpu.VMEM(adj.shape, bf16), pltpu.VMEM(margin.shape, f32), dma((2 * owners + 2,)),
        ],
        compiler_params=pltpu.CompilerParams(vmem_limit_bytes=56 * 1024 * 1024),
    )(adj, margin)
    return (margin, adj.reshape(path_rows, width))


def margin_terms(arrived, got_codes, risk_weights, correlation, funding_spread):
    path_rows = arrived.shape[0]
    cpty_count = funding_spread.shape[0]
    bucket_count = risk_weights.shape[0]
    is_filled = got_codes >= 0
    column_ids = jnp.arange(cpty_count * bucket_count, dtype=jnp.int32)
    hot_table = (got_codes[:, None] == column_ids[None, :]).astype(jnp.bfloat16)
    bucket_sums = jnp.dot(arrived, hot_table, preferred_element_type=jnp.float32)
    weighted = (
        bucket_sums.reshape(path_rows, cpty_count, bucket_count) * risk_weights[None, None, :]
    )
    rho_w = jnp.einsum("pcb,db->pcd", weighted, correlation, precision=lax.Precision.HIGHEST)
    margin_now = jnp.sqrt(jnp.sum(weighted * rho_w, axis=2) + 1e-06)
    sens_bar = (
        funding_spread[None, :, None] * risk_weights[None, None, :] * rho_w / margin_now[:, :, None]
    )
    flat_bar = sens_bar.reshape(path_rows, cpty_count * bucket_count)
    safe_codes = jnp.where(is_filled, got_codes, 0)
    slot_bar = jnp.take(flat_bar, safe_codes, axis=1) * is_filled[None, :].astype(jnp.float32)
    return (margin_now, slot_bar.astype(jnp.bfloat16))


def body(
    basis_values, coefficients, trade_cpty, trade_bucket, risk_weights, correlation, funding_spread
):
    owners = lax.axis_size("trade")
    per_device = coefficients.shape[0]
    capacity = max(2, 2 * per_device // owners)
    slot_total = owners * capacity
    cpty_count = funding_spread.shape[0]
    bucket_count = risk_weights.shape[0]
    path_rows = basis_values.shape[0]
    owner_of = trade_cpty // cpty_count
    trade_code = trade_cpty % cpty_count * bucket_count + trade_bucket
    position = jnp.arange(per_device, dtype=jnp.int32)
    same_owner = owner_of[:, None] == owner_of[None, :]
    earlier = position[None, :] < position[:, None]
    rank_in = jnp.sum((same_owner & earlier).astype(jnp.int32), axis=1)
    slot_index = owner_of * capacity + rank_in
    codes_out = jnp.full((slot_total,), -1, jnp.int32).at[slot_index].set(trade_code)
    got_codes = lax.all_to_all(codes_out, "trade", split_axis=0, concat_axis=0, tiled=True)
    delta_rows = lax.dot_general(
        basis_values, coefficients, (((1,), (1,)), ((), ())), preferred_element_type=jnp.float32
    ).astype(jnp.bfloat16)
    outgoing = jnp.zeros((path_rows, slot_total), jnp.bfloat16).at[:, slot_index].set(delta_rows)
    arrived = lax.all_to_all(outgoing, "trade", split_axis=1, concat_axis=1, tiled=True)
    margin_now, slot_bar = margin_terms(
        arrived, got_codes, risk_weights, correlation, funding_spread
    )
    returned = lax.all_to_all(slot_bar, "trade", split_axis=1, concat_axis=1, tiled=True)
    delta_bar = returned[:, slot_index]
    partial_adj = jnp.dot(delta_bar, coefficients, preferred_element_type=jnp.float32)
    basis_adjoint = lax.psum(partial_adj, "trade").astype(jnp.bfloat16)
    return (margin_now.T, basis_adjoint)


def solution(mesh):
    placed = (
        P(("date", "path"), None),
        P(("date", "trade"), None),
        P("trade"),
        P("trade"),
        P(),
        P(),
        P("trade"),
    )
    whole = split_paths if mesh.shape["trade"] == 2 * DEEP else body
    return jax.shard_map(
        whole,
        mesh=mesh,
        in_specs=placed,
        out_specs=(P("trade", ("date", "path")), P(("date", "path"), None)),
        check_vma=False,
    )
```

```python
import functools
import jax
import jax.numpy as jnp
from jax import lax
from jax.experimental import pallas as pl
from jax.experimental.pallas import tpu as pltpu
from jax.sharding import PartitionSpec as P

MESH = pl.DeviceIdType.MESH
TERMS = 2
PIECES = 2
ADJ_PIECES = 4
DEEP = 4


def split_terms(value, count):
    parts = []
    for _ in range(count):
        head = value.astype(jnp.bfloat16)
        parts.append(head)
        value = value - head.astype(jnp.float32)
    return parts


def dot_nt(a, b):
    return lax.dot_general(a, b, (((1,), (1,)), ((), ())), preferred_element_type=jnp.float32)


def dot_nn(a, b):
    return jnp.dot(a, b, preferred_element_type=jnp.float32)


def margin_kernel(
    owners, basis_in, coef_in, cpty_in, bucket_in, rw_in, corr_in, spread_in,
    adj_out, margin_out,
    held, adj_ref, margin_ref, rows_buf, cpty_buf, bucket_buf, rw_buf, corr_buf, spread_buf,
    msg, msgs, gram, cols_buf, bucket_hot, cpty_hot, cpty_cols, bar_buf, msend, mrecv,
    local, zu, zd, zr, xs, xr, cs, cr, gs, gr, ms, mr, az_u, az_d, az_r, ax_s, ax_r, outs,
):
    t = lax.axis_index("trade")
    k = lax.axis_index("path")
    z = t // 2
    x = t % 2
    per_device, width = coef_in.shape
    half = per_device // 2
    span = width // PIECES
    adj_span = width // ADJ_PIECES
    buckets = corr_in.shape[0]
    trades = owners * per_device
    path_share = rows_buf.shape[0]
    cpty_dev = mrecv.shape[1]
    cptys = owners * cpty_dev
    code_lanes = -(-per_device // 128) * 128

    def slot(zz, xx, rz, rx):
        return (xx + rx) % 2 * 4 + (zz // 2 + rz // 2) % 2 * 2 + zz % 2

    def send(src, dst, send_sem, recv_sem, to_trade, to_path):
        return pltpu.make_async_remote_copy(
            src_ref=src, dst_ref=dst, send_sem=send_sem, recv_sem=recv_sem,
            device_id={"trade": to_trade, "path": to_path}, device_id_type=MESH,
        )

    own = slot(z, x, z, x)
    small = [
        pltpu.make_async_copy(cpty_in, cpty_buf, local.at[0]),
        pltpu.make_async_copy(bucket_in, bucket_buf, local.at[1]),
        pltpu.make_async_copy(spread_in, spread_buf, local.at[2]),
    ]
    shard = [
        pltpu.make_async_copy(
            coef_in.at[pl.ds(kk * half, half)], held.at[own * 2 + kk], local.at[3 + kk]
        )
        for kk in range(2)
    ]
    rest = [
        pltpu.make_async_copy(rw_in, rw_buf, local.at[5]),
        pltpu.make_async_copy(corr_in, corr_buf, local.at[6]),
        pltpu.make_async_copy(
            basis_in.at[pl.ds(pl.multiple_of(t * path_share, 16), path_share)], rows_buf, local.at[7]
        ),
    ]
    for copy in small + shard + rest:
        copy.start()

    barrier = pltpu.get_barrier_semaphore()
    for step in range(1, owners):
        pl.semaphore_signal(
            barrier, inc=1, device_id={"trade": (t + step) % owners, "path": k}, device_id_type=MESH
        )
    pl.semaphore_signal(barrier, inc=1, device_id={"trade": t, "path": 1 - k}, device_id_type=MESH)

    for copy in small:
        copy.wait()
    msg[...] = jnp.zeros_like(msg)
    msg[:, :per_device] = (cpty_buf[...] * buckets + bucket_buf[...]).astype(jnp.float32)
    msg[:, code_lanes:code_lanes + cpty_dev] = spread_buf[...]
    msgs[0] = msg[...]
    for copy in shard:
        copy.wait()
    pl.semaphore_wait(barrier, owners)

    def msg_copy(step):
        return send(msg, msgs.at[step], gs.at[step], gr.at[step], (t + step) % owners, k)

    def piece(where, p):
        return held.at[where * 2 + k, :, pl.ds(p * span, span)]

    def hop(zz, xx, p, sems, arrive, rz, rx):
        return send(
            piece(slot(zz, xx, z, x), p), piece(slot(zz, xx, rz, rx), p),
            sems.at[zz * PIECES + p], arrive.at[zz * PIECES + p], rz * 2 + rx, k,
        )

    def up(zz, p):
        return hop(zz, x, p, zu, zr, z + 1, x)

    def down(zz, p):
        return hop(zz, x, p, zd, zr, z - 1, x)

    def across(zz, p):
        return hop(zz, x, p, xs, xr, z, 1 - x)

    def over(where, p):
        ref = piece(where, p)
        sem = where * PIECES + p
        return send(ref, ref, cs.at[sem], cr.at[sem], t, 1 - k)

    def chain_arrived(zz, p):
        ref = piece(slot(zz, x, z, x), p)
        sem = zz * PIECES + p
        send(ref, ref, zu.at[sem], zr.at[sem], z * 2 + 1 - x, k).wait_recv()

    def across_arrived(zz, p):
        ref = piece(slot(zz, 1 - x, z, x), p)
        sem = zz * PIECES + p
        send(ref, ref, xs.at[sem], xr.at[sem], z * 2 + 1 - x, k).wait_recv()

    for p in range(PIECES):
        @pl.when(z < DEEP - 1)
        def _():
            up(z, p).start()

        @pl.when(z > 0)
        def _():
            down(z, p).start()

        across(z, p).start()
        if p == 0:
            for step in range(1, owners):
                msg_copy(step).start()

    def chain_arrival(j, p):
        @pl.when(z - j >= 0)
        def _():
            zz = z - j
            chain_arrived(zz, p)

            @pl.when(z < DEEP - 1)
            def _():
                up(zz, p).start()
            across(zz, p).start()
            over(slot(zz, x, z, x), p).start()

        @pl.when(z + j < DEEP)
        def _():
            zz = z + j
            chain_arrived(zz, p)

            @pl.when(z > 0)
            def _():
                down(zz, p).start()
            across(zz, p).start()
            over(slot(zz, x, z, x), p).start()

    def across_at(zz, p):
        across_arrived(zz, p)
        over(slot(zz, 1 - x, z, x), p).start()

    def across_arrival(j, p):
        if j == 0:
            across_at(z, p)
            return

        @pl.when(z - j >= 0)
        def _():
            across_at(z - j, p)

        @pl.when(z + j < DEEP)
        def _():
            across_at(z + j, p)

    for copy in rest:
        copy.wait()
    rw_rows = jnp.broadcast_to(rw_buf[...], (buckets, buckets))
    scaled = corr_buf[...] * rw_rows * rw_rows.T
    scaled_terms = jnp.concatenate(split_terms(scaled, 3), axis=1)

    chain_arrival(1, 0)
    chain_arrival(1, 1)
    for step in range(1, owners):
        msg_copy(step).wait_recv()

    def sender(i):
        zz = (i // 2 + z // 2) % 2 * 2 + i % 2
        return zz * 2 + (i // 4 + x) % 2

    codes = jnp.concatenate(
        [msgs[(t - sender(i)) % owners][:, :per_device] for i in range(owners)], axis=1
    ).astype(jnp.int32)
    spread = jnp.concatenate(
        [msgs[(t - o) % owners][:, code_lanes:code_lanes + cpty_dev] for o in range(owners)], axis=1
    )
    cpty_row = codes // buckets
    bucket_row = codes % buckets
    bucket_hot[...] = (
        lax.broadcasted_iota(jnp.int32, (buckets, trades), 0) == bucket_row
    ).astype(jnp.float32).astype(jnp.bfloat16)
    cpty_hot[...] = (
        lax.broadcasted_iota(jnp.int32, (cptys, trades), 0) == cpty_row
    ).astype(jnp.float32).astype(jnp.bfloat16)
    cols_buf[...] = jnp.broadcast_to(codes.astype(jnp.float32), (8, trades)).T.astype(jnp.int32)

    def build(first, last):
        @pl.loop(first, last)
        def _(i):
            rows = pl.ds(pl.multiple_of(i * per_device, 16), per_device)
            code_col = cols_buf[rows, :1]
            hot = (
                lax.broadcasted_iota(jnp.int32, (per_device, buckets), 1) == code_col % buckets
            ).astype(jnp.float32).astype(jnp.bfloat16)
            same = code_col // buckets == cpty_row
            cpty_cols[rows, :] = (
                lax.broadcasted_iota(jnp.int32, (per_device, cptys), 1) == code_col // buckets
            ).astype(jnp.float32).astype(jnp.bfloat16)
            spread_out = dot_nn(hot, scaled_terms)
            picked = spread_out[:, :buckets] + (
                spread_out[:, buckets:2 * buckets] + spread_out[:, 2 * buckets:]
            )
            for first_lane in range(0, trades, buckets):
                lanes = slice(first_lane, first_lane + buckets)
                where = jnp.broadcast_to(bucket_row[:, lanes], (per_device, buckets))
                block = jnp.take_along_axis(picked, where, axis=1, mode="promise_in_bounds")
                block = jnp.where(same[:, lanes], block, 0.0)
                for term, part in enumerate(split_terms(block, TERMS)):
                    gram[term, rows, lanes] = part

    def deltas(first, last):
        for where in range(2 * first, 2 * last):
            for p in range(PIECES):
                if where < 2:
                    @pl.when(where != own)
                    def _():
                        over(where, p).wait_recv()
                else:
                    over(where, p).wait_recv()
        rows = slice(first * 2 * per_device, last * 2 * per_device)
        coef_rows = held[first * 4:last * 4].reshape((last - first) * 2 * per_device, width)
        delta = dot_nt(rows_buf[...], coef_rows).astype(jnp.bfloat16)
        out = dot_nn(delta, gram[TERMS - 1, rows, :])
        for term in range(TERMS - 2, -1, -1):
            out = out + dot_nn(delta, gram[term, rows, :])
        return delta.astype(jnp.float32), out

    chain_arrival(2, 0)
    across_arrival(0, 0)
    across_arrival(0, 1)
    build(0, 1)
    chain_arrival(2, 1)
    build(1, 2)
    chain_arrival(3, 0)
    build(2, 3)
    chain_arrival(3, 1)
    across_arrival(1, 0)
    build(3, 4)
    across_arrival(1, 1)
    build(4, 6)
    across_arrival(2, 0)
    build(6, 8)
    across_arrival(2, 1)
    d0, v0 = deltas(0, 2)
    across_arrival(3, 0)
    across_arrival(3, 1)
    d2, v2 = deltas(2, 3)
    early = v0 + v2
    d3, v3 = deltas(3, 4)
    v = early + v3

    delta_all = jnp.concatenate([d0, d2, d3], axis=1)
    terms = jnp.concatenate(split_terms(delta_all * v, 3), axis=0)
    sums = dot_nn(terms, cpty_cols[...])
    quad = sums[:path_share] + (sums[path_share:2 * path_share] + sums[2 * path_share:])
    margin = jnp.sqrt(quad + 1e-06)
    ratio_terms = jnp.concatenate(split_terms(spread / margin, 3), axis=0)
    spans = dot_nn(ratio_terms, cpty_hot[...])
    ratio = spans[:path_share] + (spans[path_share:2 * path_share] + spans[2 * path_share:])
    bar_buf[...] = (ratio * v).astype(jnp.bfloat16)

    def a_piece(zz, xx, p):
        return adj_ref.at[zz * 2 + xx, :, pl.ds(p * adj_span, adj_span)]

    def a_up(zz, p):
        ref = a_piece(zz, x, p)
        sem = zz * ADJ_PIECES + p
        return send(ref, ref, az_u.at[sem], az_r.at[sem], (z + 1) * 2 + x, k)

    def a_down(zz, p):
        ref = a_piece(zz, x, p)
        sem = zz * ADJ_PIECES + p
        return send(ref, ref, az_d.at[sem], az_r.at[sem], (z - 1) * 2 + x, k)

    def a_across(zz, xx, p):
        ref = a_piece(zz, xx, p)
        sem = zz * ADJ_PIECES + p
        return send(ref, ref, ax_s.at[sem], ax_r.at[sem], z * 2 + 1 - x, k)

    def out_copy(where):
        return pltpu.make_async_copy(adj_ref.at[where], adj_out.at[where], outs.at[where])

    for p in range(ADJ_PIECES):
        if p % (ADJ_PIECES // PIECES) == 0:
            wide = slice(p * adj_span, p * adj_span + span)
            coef_all = held[:, :, wide].reshape(trades, span)
            adj_ref[t, :, wide] = dot_nn(bar_buf[...], coef_all).astype(jnp.bfloat16)

        @pl.when(z < DEEP - 1)
        def _():
            a_up(z, p).start()

        @pl.when(z > 0)
        def _():
            a_down(z, p).start()

        a_across(z, x, p).start()
    out_copy(t).start()

    flipped = jnp.concatenate([margin, margin], axis=0).T[:, :path_share]
    msend[...] = flipped.reshape(owners, cpty_dev, path_share)

    def margin_copy(step):
        to = (t + step) % owners
        return send(msend.at[to], mrecv.at[step], ms.at[step], mr.at[step], to, k)

    for step in range(1, owners):
        margin_copy(step).start()

    for j in range(1, DEEP):
        for p in range(ADJ_PIECES):
            @pl.when(z - j >= 0)
            def _():
                a_up(z - j, p).wait_recv()

                @pl.when(z < DEEP - 1)
                def _():
                    a_up(z - j, p).start()
                a_across(z - j, x, p).start()

            @pl.when(z + j < DEEP)
            def _():
                a_down(z + j, p).wait_recv()

                @pl.when(z > 0)
                def _():
                    a_down(z + j, p).start()
                a_across(z + j, x, p).start()

        @pl.when(z - j >= 0)
        def _():
            out_copy((z - j) * 2 + x).start()

        @pl.when(z + j < DEEP)
        def _():
            out_copy((z + j) * 2 + x).start()

    for step in range(1, owners):
        margin_copy(step).wait_recv()
    mrecv[0] = msend[t]
    for first in range(0, owners, 2):
        pair = [mrecv[(t - o) % owners] for o in (first, first + 1)]
        margin_ref[:, first * path_share:(first + 2) * path_share] = jnp.concatenate(pair, axis=1)
    margin_done = pltpu.make_async_copy(margin_ref, margin_out, local.at[0])
    margin_done.start()

    def adj_across(zz):
        for p in range(ADJ_PIECES):
            a_across(zz, 1 - x, p).wait_recv()
        out_copy(zz * 2 + 1 - x).start()

    adj_across(z)
    for j in range(1, DEEP):
        @pl.when(z - j >= 0)
        def _():
            adj_across(z - j)

        @pl.when(z + j < DEEP)
        def _():
            adj_across(z + j)

    for step in range(1, owners):
        msg_copy(step).wait_send()
        margin_copy(step).wait_send()
    for p in range(PIECES):
        for where in range(owners):
            @pl.when(where != own)
            def _():
                over(where, p).wait_send()
        for zz in range(DEEP):
            across(zz, p).wait_send()

            @pl.when((zz <= z) & (z < DEEP - 1))
            def _():
                up(zz, p).wait_send()

            @pl.when((zz >= z) & (z > 0))
            def _():
                down(zz, p).wait_send()
    for p in range(ADJ_PIECES):
        for zz in range(DEEP):
            a_across(zz, x, p).wait_send()

            @pl.when((zz <= z) & (z < DEEP - 1))
            def _():
                a_up(zz, p).wait_send()

            @pl.when((zz >= z) & (z > 0))
            def _():
                a_down(zz, p).wait_send()
    margin_done.wait()
    for where in range(owners):
        out_copy(where).wait()


def hand_over(adj_in, margin_in, adj_out, margin_out, adj_held, margin_held, sems):
    count = adj_in.shape[0]
    legs = [(adj_in.at[i], adj_held.at[i], adj_out.at[i]) for i in range(count)]
    legs.append((margin_in, margin_held, margin_out))
    reads = [pltpu.make_async_copy(a, b, sems.at[i]) for i, (a, b, _) in enumerate(legs)]
    writes = [
        pltpu.make_async_copy(b, c, sems.at[count + 1 + i]) for i, (_, b, c) in enumerate(legs)
    ]
    for copy in reads:
        copy.start()
    for read, write in zip(reads, writes):
        read.wait()
        write.start()
    for copy in writes:
        copy.wait()


def split_paths(
    basis_values, coefficients, trade_cpty, trade_bucket, risk_weights, correlation, funding_spread
):
    owners = lax.axis_size("trade")
    per_device, width = coefficients.shape
    cpty_dev = funding_spread.shape[0]
    buckets = risk_weights.shape[0]
    path_rows = basis_values.shape[0]
    path_share = path_rows // owners
    trades = owners * per_device
    cptys = owners * cpty_dev
    hbm = pl.BlockSpec(memory_space=pltpu.HBM)
    dma = pltpu.SemaphoreType.DMA
    f32, i32, bf16 = jnp.float32, jnp.int32, jnp.bfloat16
    msg_lanes = -(-per_device // 128) * 128 + 128
    pieces = DEEP * PIECES
    adj_pieces = DEEP * ADJ_PIECES
    adj, margin = pl.pallas_call(
        functools.partial(margin_kernel, owners),
        out_shape=(
            jax.ShapeDtypeStruct((owners, path_share, width), bf16),
            jax.ShapeDtypeStruct((cpty_dev, path_rows), f32),
        ),
        in_specs=[hbm] * 7,
        out_specs=(hbm, hbm),
        scratch_shapes=[
            pltpu.VMEM((owners * 2, per_device // 2, width), bf16),
            pltpu.VMEM((owners, path_share, width), bf16),
            pltpu.VMEM((cpty_dev, path_rows), f32),
            pltpu.VMEM((path_share, width), bf16),
            pltpu.VMEM((1, per_device), i32),
            pltpu.VMEM((1, per_device), i32),
            pltpu.VMEM((1, buckets), f32),
            pltpu.VMEM((buckets, buckets), f32),
            pltpu.VMEM((1, cpty_dev), f32),
            pltpu.VMEM((1, msg_lanes), f32),
            pltpu.VMEM((owners, 1, msg_lanes), f32),
            pltpu.VMEM((TERMS, trades, trades), bf16),
            pltpu.VMEM((trades, 8), i32),
            pltpu.VMEM((buckets, trades), bf16),
            pltpu.VMEM((cptys, trades), bf16),
            pltpu.VMEM((trades, cptys), bf16),
            pltpu.VMEM((path_share, trades), bf16),
            pltpu.VMEM((owners, cpty_dev, path_share), f32),
            pltpu.VMEM((owners, cpty_dev, path_share), f32),
            dma((8,)), dma((pieces,)), dma((pieces,)), dma((pieces,)), dma((pieces,)), dma((pieces,)),
            dma((owners * PIECES,)), dma((owners * PIECES,)),
            dma((owners,)), dma((owners,)), dma((owners,)), dma((owners,)),
            dma((adj_pieces,)), dma((adj_pieces,)), dma((adj_pieces,)), dma((adj_pieces,)),
            dma((adj_pieces,)), dma((owners,)),
        ],
        compiler_params=pltpu.CompilerParams(
            collective_id=0, has_side_effects=True, vmem_limit_bytes=56 * 1024 * 1024
        ),
    )(
        basis_values, coefficients, trade_cpty[None, :], trade_bucket[None, :],
        risk_weights[None, :], correlation, funding_spread[None, :],
    )
    adj, margin = pl.pallas_call(
        hand_over,
        out_shape=(
            jax.ShapeDtypeStruct(adj.shape, bf16), jax.ShapeDtypeStruct(margin.shape, f32),
        ),
        in_specs=[hbm, hbm],
        out_specs=(hbm, hbm),
        scratch_shapes=[
            pltpu.VMEM(adj.shape, bf16), pltpu.VMEM(margin.shape, f32), dma((2 * owners + 2,)),
        ],
        compiler_params=pltpu.CompilerParams(vmem_limit_bytes=56 * 1024 * 1024),
    )(adj, margin)
    return (margin, adj.reshape(path_rows, width))


def margin_terms(arrived, got_codes, risk_weights, correlation, funding_spread):
    path_rows = arrived.shape[0]
    cpty_count = funding_spread.shape[0]
    bucket_count = risk_weights.shape[0]
    is_filled = got_codes >= 0
    column_ids = jnp.arange(cpty_count * bucket_count, dtype=jnp.int32)
    hot_table = (got_codes[:, None] == column_ids[None, :]).astype(jnp.bfloat16)
    bucket_sums = jnp.dot(arrived, hot_table, preferred_element_type=jnp.float32)
    weighted = (
        bucket_sums.reshape(path_rows, cpty_count, bucket_count) * risk_weights[None, None, :]
    )
    rho_w = jnp.einsum("pcb,db->pcd", weighted, correlation, precision=lax.Precision.HIGHEST)
    margin_now = jnp.sqrt(jnp.sum(weighted * rho_w, axis=2) + 1e-06)
    sens_bar = (
        funding_spread[None, :, None] * risk_weights[None, None, :] * rho_w / margin_now[:, :, None]
    )
    flat_bar = sens_bar.reshape(path_rows, cpty_count * bucket_count)
    safe_codes = jnp.where(is_filled, got_codes, 0)
    slot_bar = jnp.take(flat_bar, safe_codes, axis=1) * is_filled[None, :].astype(jnp.float32)
    return (margin_now, slot_bar.astype(jnp.bfloat16))


def body(
    basis_values, coefficients, trade_cpty, trade_bucket, risk_weights, correlation, funding_spread
):
    owners = lax.axis_size("trade")
    per_device = coefficients.shape[0]
    capacity = max(2, 2 * per_device // owners)
    slot_total = owners * capacity
    cpty_count = funding_spread.shape[0]
    bucket_count = risk_weights.shape[0]
    path_rows = basis_values.shape[0]
    owner_of = trade_cpty // cpty_count
    trade_code = trade_cpty % cpty_count * bucket_count + trade_bucket
    position = jnp.arange(per_device, dtype=jnp.int32)
    same_owner = owner_of[:, None] == owner_of[None, :]
    earlier = position[None, :] < position[:, None]
    rank_in = jnp.sum((same_owner & earlier).astype(jnp.int32), axis=1)
    slot_index = owner_of * capacity + rank_in
    codes_out = jnp.full((slot_total,), -1, jnp.int32).at[slot_index].set(trade_code)
    got_codes = lax.all_to_all(codes_out, "trade", split_axis=0, concat_axis=0, tiled=True)
    delta_rows = lax.dot_general(
        basis_values, coefficients, (((1,), (1,)), ((), ())), preferred_element_type=jnp.float32
    ).astype(jnp.bfloat16)
    outgoing = jnp.zeros((path_rows, slot_total), jnp.bfloat16).at[:, slot_index].set(delta_rows)
    arrived = lax.all_to_all(outgoing, "trade", split_axis=1, concat_axis=1, tiled=True)
    margin_now, slot_bar = margin_terms(
        arrived, got_codes, risk_weights, correlation, funding_spread
    )
    returned = lax.all_to_all(slot_bar, "trade", split_axis=1, concat_axis=1, tiled=True)
    delta_bar = returned[:, slot_index]
    partial_adj = jnp.dot(delta_bar, coefficients, preferred_element_type=jnp.float32)
    basis_adjoint = lax.psum(partial_adj, "trade").astype(jnp.bfloat16)
    return (margin_now.T, basis_adjoint)


def solution(mesh):
    placed = (
        P(("date", "path"), None),
        P(("date", "trade"), None),
        P("trade"),
        P("trade"),
        P(),
        P(),
        P("trade"),
    )
    whole = split_paths if mesh.shape["trade"] == 2 * DEEP else body
    return jax.shard_map(
        whole,
        mesh=mesh,
        in_specs=placed,
        out_specs=(P("trade", ("date", "path")), P(("date", "path"), None)),
        check_vma=False,
    )
```

```python
import functools
import jax
import jax.numpy as jnp
from jax import lax
from jax.experimental import pallas as pl
from jax.experimental.pallas import tpu as pltpu
from jax.sharding import PartitionSpec as P

MESH = pl.DeviceIdType.MESH
TERMS = 2
PIECES = 2
ADJ_PIECES = 4
DEEP = 4


def split_terms(value, count):
    parts = []
    for _ in range(count):
        head = value.astype(jnp.bfloat16)
        parts.append(head)
        value = value - head.astype(jnp.float32)
    return parts


def dot_nt(a, b):
    return lax.dot_general(a, b, (((1,), (1,)), ((), ())), preferred_element_type=jnp.float32)


def dot_nn(a, b):
    return jnp.dot(a, b, preferred_element_type=jnp.float32)


def margin_kernel(
    owners, basis_in, coef_in, cpty_in, bucket_in, rw_in, corr_in, spread_in,
    adj_out, margin_out,
    held, adj_ref, margin_ref, rows_buf, cpty_buf, bucket_buf, rw_buf, corr_buf, spread_buf,
    msg, msgs, gram, cols_buf, bucket_hot, cpty_hot, cpty_cols, bar_buf, msend, mrecv,
    local, zu, zd, zr, xs, xr, cs, cr, gs, gr, ms, mr, az_u, az_d, az_r, ax_s, ax_r, outs,
):
    t = lax.axis_index("trade")
    k = lax.axis_index("path")
    z = t // 2
    x = t % 2
    per_device, width = coef_in.shape
    half = per_device // 2
    span = width // PIECES
    adj_span = width // ADJ_PIECES
    buckets = corr_in.shape[0]
    trades = owners * per_device
    path_share = rows_buf.shape[0]
    cpty_dev = mrecv.shape[1]
    cptys = owners * cpty_dev
    code_lanes = -(-per_device // 128) * 128

    def slot(zz, xx, rz, rx):
        return (xx + rx) % 2 * 4 + (zz // 2 + rz // 2) % 2 * 2 + (zz + rz // 2) % 2

    def send(src, dst, send_sem, recv_sem, to_trade, to_path):
        return pltpu.make_async_remote_copy(
            src_ref=src, dst_ref=dst, send_sem=send_sem, recv_sem=recv_sem,
            device_id={"trade": to_trade, "path": to_path}, device_id_type=MESH,
        )

    own = slot(z, x, z, x)
    small = [
        pltpu.make_async_copy(cpty_in, cpty_buf, local.at[0]),
        pltpu.make_async_copy(bucket_in, bucket_buf, local.at[1]),
        pltpu.make_async_copy(spread_in, spread_buf, local.at[2]),
    ]
    shard = [
        pltpu.make_async_copy(
            coef_in.at[pl.ds(kk * half, half)], held.at[own * 2 + kk], local.at[3 + kk]
        )
        for kk in range(2)
    ]
    rest = [
        pltpu.make_async_copy(rw_in, rw_buf, local.at[5]),
        pltpu.make_async_copy(corr_in, corr_buf, local.at[6]),
        pltpu.make_async_copy(
            basis_in.at[pl.ds(pl.multiple_of(t * path_share, 16), path_share)], rows_buf, local.at[7]
        ),
    ]
    for copy in small + shard + rest:
        copy.start()

    barrier = pltpu.get_barrier_semaphore()
    for step in range(1, owners):
        pl.semaphore_signal(
            barrier, inc=1, device_id={"trade": (t + step) % owners, "path": k}, device_id_type=MESH
        )
    pl.semaphore_signal(barrier, inc=1, device_id={"trade": t, "path": 1 - k}, device_id_type=MESH)

    for copy in small:
        copy.wait()
    msg[...] = jnp.zeros_like(msg)
    msg[:, :per_device] = (cpty_buf[...] * buckets + bucket_buf[...]).astype(jnp.float32)
    msg[:, code_lanes:code_lanes + cpty_dev] = spread_buf[...]
    msgs[0] = msg[...]
    for copy in shard:
        copy.wait()
    pl.semaphore_wait(barrier, owners)

    def msg_copy(step):
        return send(msg, msgs.at[step], gs.at[step], gr.at[step], (t + step) % owners, k)

    def piece(where, p):
        return held.at[where * 2 + k, :, pl.ds(p * span, span)]

    def hop(zz, xx, p, sems, arrive, rz, rx):
        return send(
            piece(slot(zz, xx, z, x), p), piece(slot(zz, xx, rz, rx), p),
            sems.at[zz * PIECES + p], arrive.at[zz * PIECES + p], rz * 2 + rx, k,
        )

    def up(zz, p):
        return hop(zz, x, p, zu, zr, z + 1, x)

    def down(zz, p):
        return hop(zz, x, p, zd, zr, z - 1, x)

    def across(zz, p):
        return hop(zz, x, p, xs, xr, z, 1 - x)

    def over(where, p):
        ref = piece(where, p)
        sem = where * PIECES + p
        return send(ref, ref, cs.at[sem], cr.at[sem], t, 1 - k)

    def chain_arrived(zz, p):
        ref = piece(slot(zz, x, z, x), p)
        sem = zz * PIECES + p
        send(ref, ref, zu.at[sem], zr.at[sem], z * 2 + 1 - x, k).wait_recv()

    def across_arrived(zz, p):
        ref = piece(slot(zz, 1 - x, z, x), p)
        sem = zz * PIECES + p
        send(ref, ref, xs.at[sem], xr.at[sem], z * 2 + 1 - x, k).wait_recv()

    for p in range(PIECES):
        @pl.when(z < DEEP - 1)
        def _():
            up(z, p).start()

        @pl.when(z > 0)
        def _():
            down(z, p).start()

        across(z, p).start()
        if p == 0:
            for step in range(1, owners):
                msg_copy(step).start()

    def chain_arrival(j, p):
        @pl.when(z - j >= 0)
        def _():
            zz = z - j
            chain_arrived(zz, p)

            @pl.when(z < DEEP - 1)
            def _():
                up(zz, p).start()
            across(zz, p).start()
            over(slot(zz, x, z, x), p).start()

        @pl.when(z + j < DEEP)
        def _():
            zz = z + j
            chain_arrived(zz, p)

            @pl.when(z > 0)
            def _():
                down(zz, p).start()
            across(zz, p).start()
            over(slot(zz, x, z, x), p).start()

    def across_at(zz, p):
        across_arrived(zz, p)
        over(slot(zz, 1 - x, z, x), p).start()

    def across_arrival(j, p):
        if j == 0:
            across_at(z, p)
            return

        @pl.when(z - j >= 0)
        def _():
            across_at(z - j, p)

        @pl.when(z + j < DEEP)
        def _():
            across_at(z + j, p)

    for copy in rest:
        copy.wait()
    rw_rows = jnp.broadcast_to(rw_buf[...], (buckets, buckets))
    scaled = corr_buf[...] * rw_rows * rw_rows.T
    scaled_terms = jnp.concatenate(split_terms(scaled, TERMS), axis=1)

    chain_arrival(1, 0)
    chain_arrival(1, 1)
    for step in range(1, owners):
        msg_copy(step).wait_recv()

    def sender(i):
        zz = (i // 2 + z // 2) % 2 * 2 + (i + z // 2) % 2
        return zz * 2 + (i // 4 + x) % 2

    codes = jnp.concatenate(
        [msgs[(t - sender(i)) % owners][:, :per_device] for i in range(owners)], axis=1
    ).astype(jnp.int32)
    spread = jnp.concatenate(
        [msgs[(t - o) % owners][:, code_lanes:code_lanes + cpty_dev] for o in range(owners)], axis=1
    )
    cpty_row = codes // buckets
    bucket_row = codes % buckets
    bucket_hot[...] = (
        lax.broadcasted_iota(jnp.int32, (buckets, trades), 0) == bucket_row
    ).astype(jnp.float32).astype(jnp.bfloat16)
    cpty_hot[...] = (
        lax.broadcasted_iota(jnp.int32, (cptys, trades), 0) == cpty_row
    ).astype(jnp.float32).astype(jnp.bfloat16)
    cols_buf[...] = jnp.broadcast_to(codes.astype(jnp.float32), (8, trades)).T.astype(jnp.int32)

    block_rows = 2 * per_device

    def build(first, last):
        @pl.loop(first, last)
        def _(i):
            rows = pl.ds(pl.multiple_of(i * block_rows, 16), block_rows)
            code_col = cols_buf[rows, :1]
            hot = (
                lax.broadcasted_iota(jnp.int32, (block_rows, buckets), 1) == code_col % buckets
            ).astype(jnp.float32).astype(jnp.bfloat16)
            same = code_col // buckets == cpty_row
            cpty_cols[rows, :] = (
                lax.broadcasted_iota(jnp.int32, (block_rows, cptys), 1) == code_col // buckets
            ).astype(jnp.float32).astype(jnp.bfloat16)
            picked = dot_nn(hot, scaled_terms).astype(jnp.bfloat16)
            stacked = jnp.concatenate(
                [picked[:, term * buckets:(term + 1) * buckets] for term in range(TERMS)], axis=0
            )
            blocks = dot_nn(stacked, bucket_hot[...])
            for term in range(TERMS):
                block = blocks[term * block_rows:(term + 1) * block_rows]
                gram[term, rows, :] = jnp.where(same, block, 0.0).astype(jnp.bfloat16)

    def deltas(first, last):
        for where in range(first, last):
            for p in range(PIECES):
                if where < 2:
                    @pl.when(where != own)
                    def _():
                        over(where, p).wait_recv()
                else:
                    over(where, p).wait_recv()
        coef_rows = held[first * 2:last * 2].reshape((last - first) * per_device, width)
        return dot_nt(rows_buf[...], coef_rows)

    def spans_of(delta, first, last):
        out = dot_nn(delta, gram[TERMS - 1, first:last, :])
        for term in range(TERMS - 2, -1, -1):
            out = out + dot_nn(delta, gram[term, first:last, :])
        return out

    chain_arrival(2, 0)
    across_arrival(0, 0)
    across_arrival(0, 1)
    build(0, 1)
    chain_arrival(2, 1)
    chain_arrival(3, 0)
    build(1, 2)
    chain_arrival(3, 1)
    across_arrival(1, 0)
    across_arrival(1, 1)
    build(2, 3)
    across_arrival(2, 0)
    build(3, 4)
    across_arrival(2, 1)
    cut, tail = trades * 2 // 5, trades * 4 // 5
    d0 = deltas(0, 4)
    v = spans_of(d0[:, :cut].astype(jnp.bfloat16), 0, cut)
    d1 = deltas(4, 7)
    across_arrival(3, 0)
    middle = jnp.concatenate([d0[:, cut:], d1], axis=1)
    v = v + spans_of(middle[:, :tail - cut].astype(jnp.bfloat16), cut, tail)
    across_arrival(3, 1)
    d2 = deltas(7, 8)
    delta_all = jnp.concatenate([d0, d1, d2], axis=1).astype(jnp.bfloat16)
    v = v + spans_of(delta_all[:, tail:], tail, trades)
    delta_all = delta_all.astype(jnp.float32)

    terms = jnp.concatenate(split_terms(delta_all * v, 3), axis=0)
    sums = dot_nn(terms, cpty_cols[...])
    quad = sums[:path_share] + (sums[path_share:2 * path_share] + sums[2 * path_share:])
    margin = jnp.sqrt(quad + 1e-06)
    ratio_terms = jnp.concatenate(split_terms(spread / margin, 3), axis=0)
    spans = dot_nn(ratio_terms, cpty_hot[...])
    ratio = spans[:path_share] + (spans[path_share:2 * path_share] + spans[2 * path_share:])
    bar_buf[...] = (ratio * v).astype(jnp.bfloat16)

    def a_piece(zz, xx, p):
        return adj_ref.at[zz * 2 + xx, :, pl.ds(p * adj_span, adj_span)]

    def a_up(zz, p):
        ref = a_piece(zz, x, p)
        sem = zz * ADJ_PIECES + p
        return send(ref, ref, az_u.at[sem], az_r.at[sem], (z + 1) * 2 + x, k)

    def a_down(zz, p):
        ref = a_piece(zz, x, p)
        sem = zz * ADJ_PIECES + p
        return send(ref, ref, az_d.at[sem], az_r.at[sem], (z - 1) * 2 + x, k)

    def a_across(zz, xx, p):
        ref = a_piece(zz, xx, p)
        sem = zz * ADJ_PIECES + p
        return send(ref, ref, ax_s.at[sem], ax_r.at[sem], z * 2 + 1 - x, k)

    def out_copy(where):
        return pltpu.make_async_copy(adj_ref.at[where], adj_out.at[where], outs.at[where])

    for p in range(ADJ_PIECES):
        if p % (ADJ_PIECES // PIECES) == 0:
            wide = slice(p * adj_span, p * adj_span + span)
            coef_all = held[:, :, wide].reshape(trades, span)
            adj_ref[t, :, wide] = dot_nn(bar_buf[...], coef_all).astype(jnp.bfloat16)

        @pl.when(z < DEEP - 1)
        def _():
            a_up(z, p).start()

        @pl.when(z > 0)
        def _():
            a_down(z, p).start()

        a_across(z, x, p).start()
    out_copy(t).start()

    flipped = jnp.concatenate([margin, margin], axis=0).T[:, :path_share]
    msend[...] = flipped.reshape(owners, cpty_dev, path_share)

    def margin_copy(step):
        to = (t + step) % owners
        return send(msend.at[to], mrecv.at[step], ms.at[step], mr.at[step], to, k)

    for step in range(1, owners):
        margin_copy(step).start()

    for j in range(1, DEEP):
        for p in range(ADJ_PIECES):
            @pl.when(z - j >= 0)
            def _():
                a_up(z - j, p).wait_recv()

                @pl.when(z < DEEP - 1)
                def _():
                    a_up(z - j, p).start()
                a_across(z - j, x, p).start()

            @pl.when(z + j < DEEP)
            def _():
                a_down(z + j, p).wait_recv()

                @pl.when(z > 0)
                def _():
                    a_down(z + j, p).start()
                a_across(z + j, x, p).start()

        @pl.when(z - j >= 0)
        def _():
            out_copy((z - j) * 2 + x).start()

        @pl.when(z + j < DEEP)
        def _():
            out_copy((z + j) * 2 + x).start()

    for step in range(1, owners):
        margin_copy(step).wait_recv()
    mrecv[0] = msend[t]
    for first in range(0, owners, 2):
        pair = [mrecv[(t - o) % owners] for o in (first, first + 1)]
        margin_ref[:, first * path_share:(first + 2) * path_share] = jnp.concatenate(pair, axis=1)
    margin_done = pltpu.make_async_copy(margin_ref, margin_out, local.at[0])
    margin_done.start()

    def adj_across(zz):
        for p in range(ADJ_PIECES):
            a_across(zz, 1 - x, p).wait_recv()
        out_copy(zz * 2 + 1 - x).start()

    adj_across(z)
    for j in range(1, DEEP):
        @pl.when(z - j >= 0)
        def _():
            adj_across(z - j)

        @pl.when(z + j < DEEP)
        def _():
            adj_across(z + j)

    for step in range(1, owners):
        msg_copy(step).wait_send()
        margin_copy(step).wait_send()
    for p in range(PIECES):
        for where in range(owners):
            @pl.when(where != own)
            def _():
                over(where, p).wait_send()
        for zz in range(DEEP):
            across(zz, p).wait_send()

            @pl.when((zz <= z) & (z < DEEP - 1))
            def _():
                up(zz, p).wait_send()

            @pl.when((zz >= z) & (z > 0))
            def _():
                down(zz, p).wait_send()
    for p in range(ADJ_PIECES):
        for zz in range(DEEP):
            a_across(zz, x, p).wait_send()

            @pl.when((zz <= z) & (z < DEEP - 1))
            def _():
                a_up(zz, p).wait_send()

            @pl.when((zz >= z) & (z > 0))
            def _():
                a_down(zz, p).wait_send()
    margin_done.wait()
    for where in range(owners):
        out_copy(where).wait()


def hand_over(adj_in, margin_in, adj_out, margin_out, adj_held, margin_held, sems):
    count = adj_in.shape[0]
    legs = [(adj_in.at[i], adj_held.at[i], adj_out.at[i]) for i in range(count)]
    legs.append((margin_in, margin_held, margin_out))
    reads = [pltpu.make_async_copy(a, b, sems.at[i]) for i, (a, b, _) in enumerate(legs)]
    writes = [
        pltpu.make_async_copy(b, c, sems.at[count + 1 + i]) for i, (_, b, c) in enumerate(legs)
    ]
    for copy in reads:
        copy.start()
    for read, write in zip(reads, writes):
        read.wait()
        write.start()
    for copy in writes:
        copy.wait()


def split_paths(
    basis_values, coefficients, trade_cpty, trade_bucket, risk_weights, correlation, funding_spread
):
    owners = lax.axis_size("trade")
    per_device, width = coefficients.shape
    cpty_dev = funding_spread.shape[0]
    buckets = risk_weights.shape[0]
    path_rows = basis_values.shape[0]
    path_share = path_rows // owners
    trades = owners * per_device
    cptys = owners * cpty_dev
    hbm = pl.BlockSpec(memory_space=pltpu.HBM)
    dma = pltpu.SemaphoreType.DMA
    f32, i32, bf16 = jnp.float32, jnp.int32, jnp.bfloat16
    msg_lanes = -(-per_device // 128) * 128 + 128
    pieces = DEEP * PIECES
    adj_pieces = DEEP * ADJ_PIECES
    adj, margin = pl.pallas_call(
        functools.partial(margin_kernel, owners),
        out_shape=(
            jax.ShapeDtypeStruct((owners, path_share, width), bf16),
            jax.ShapeDtypeStruct((cpty_dev, path_rows), f32),
        ),
        in_specs=[hbm] * 7,
        out_specs=(hbm, hbm),
        scratch_shapes=[
            pltpu.VMEM((owners * 2, per_device // 2, width), bf16),
            pltpu.VMEM((owners, path_share, width), bf16),
            pltpu.VMEM((cpty_dev, path_rows), f32),
            pltpu.VMEM((path_share, width), bf16),
            pltpu.VMEM((1, per_device), i32),
            pltpu.VMEM((1, per_device), i32),
            pltpu.VMEM((1, buckets), f32),
            pltpu.VMEM((buckets, buckets), f32),
            pltpu.VMEM((1, cpty_dev), f32),
            pltpu.VMEM((1, msg_lanes), f32),
            pltpu.VMEM((owners, 1, msg_lanes), f32),
            pltpu.VMEM((TERMS, trades, trades), bf16),
            pltpu.VMEM((trades, 8), i32),
            pltpu.VMEM((buckets, trades), bf16),
            pltpu.VMEM((cptys, trades), bf16),
            pltpu.VMEM((trades, cptys), bf16),
            pltpu.VMEM((path_share, trades), bf16),
            pltpu.VMEM((owners, cpty_dev, path_share), f32),
            pltpu.VMEM((owners, cpty_dev, path_share), f32),
            dma((8,)), dma((pieces,)), dma((pieces,)), dma((pieces,)), dma((pieces,)), dma((pieces,)),
            dma((owners * PIECES,)), dma((owners * PIECES,)),
            dma((owners,)), dma((owners,)), dma((owners,)), dma((owners,)),
            dma((adj_pieces,)), dma((adj_pieces,)), dma((adj_pieces,)), dma((adj_pieces,)),
            dma((adj_pieces,)), dma((owners,)),
        ],
        compiler_params=pltpu.CompilerParams(
            collective_id=0, has_side_effects=True, vmem_limit_bytes=56 * 1024 * 1024
        ),
    )(
        basis_values, coefficients, trade_cpty[None, :], trade_bucket[None, :],
        risk_weights[None, :], correlation, funding_spread[None, :],
    )
    adj, margin = pl.pallas_call(
        hand_over,
        out_shape=(
            jax.ShapeDtypeStruct(adj.shape, bf16), jax.ShapeDtypeStruct(margin.shape, f32),
        ),
        in_specs=[hbm, hbm],
        out_specs=(hbm, hbm),
        scratch_shapes=[
            pltpu.VMEM(adj.shape, bf16), pltpu.VMEM(margin.shape, f32), dma((2 * owners + 2,)),
        ],
        compiler_params=pltpu.CompilerParams(vmem_limit_bytes=56 * 1024 * 1024),
    )(adj, margin)
    return (margin, adj.reshape(path_rows, width))


def margin_terms(arrived, got_codes, risk_weights, correlation, funding_spread):
    path_rows = arrived.shape[0]
    cpty_count = funding_spread.shape[0]
    bucket_count = risk_weights.shape[0]
    is_filled = got_codes >= 0
    column_ids = jnp.arange(cpty_count * bucket_count, dtype=jnp.int32)
    hot_table = (got_codes[:, None] == column_ids[None, :]).astype(jnp.bfloat16)
    bucket_sums = jnp.dot(arrived, hot_table, preferred_element_type=jnp.float32)
    weighted = (
        bucket_sums.reshape(path_rows, cpty_count, bucket_count) * risk_weights[None, None, :]
    )
    rho_w = jnp.einsum("pcb,db->pcd", weighted, correlation, precision=lax.Precision.HIGHEST)
    margin_now = jnp.sqrt(jnp.sum(weighted * rho_w, axis=2) + 1e-06)
    sens_bar = (
        funding_spread[None, :, None] * risk_weights[None, None, :] * rho_w / margin_now[:, :, None]
    )
    flat_bar = sens_bar.reshape(path_rows, cpty_count * bucket_count)
    safe_codes = jnp.where(is_filled, got_codes, 0)
    slot_bar = jnp.take(flat_bar, safe_codes, axis=1) * is_filled[None, :].astype(jnp.float32)
    return (margin_now, slot_bar.astype(jnp.bfloat16))


def body(
    basis_values, coefficients, trade_cpty, trade_bucket, risk_weights, correlation, funding_spread
):
    owners = lax.axis_size("trade")
    per_device = coefficients.shape[0]
    capacity = max(2, 2 * per_device // owners)
    slot_total = owners * capacity
    cpty_count = funding_spread.shape[0]
    bucket_count = risk_weights.shape[0]
    path_rows = basis_values.shape[0]
    owner_of = trade_cpty // cpty_count
    trade_code = trade_cpty % cpty_count * bucket_count + trade_bucket
    position = jnp.arange(per_device, dtype=jnp.int32)
    same_owner = owner_of[:, None] == owner_of[None, :]
    earlier = position[None, :] < position[:, None]
    rank_in = jnp.sum((same_owner & earlier).astype(jnp.int32), axis=1)
    slot_index = owner_of * capacity + rank_in
    codes_out = jnp.full((slot_total,), -1, jnp.int32).at[slot_index].set(trade_code)
    got_codes = lax.all_to_all(codes_out, "trade", split_axis=0, concat_axis=0, tiled=True)
    delta_rows = lax.dot_general(
        basis_values, coefficients, (((1,), (1,)), ((), ())), preferred_element_type=jnp.float32
    ).astype(jnp.bfloat16)
    outgoing = jnp.zeros((path_rows, slot_total), jnp.bfloat16).at[:, slot_index].set(delta_rows)
    arrived = lax.all_to_all(outgoing, "trade", split_axis=1, concat_axis=1, tiled=True)
    margin_now, slot_bar = margin_terms(
        arrived, got_codes, risk_weights, correlation, funding_spread
    )
    returned = lax.all_to_all(slot_bar, "trade", split_axis=1, concat_axis=1, tiled=True)
    delta_bar = returned[:, slot_index]
    partial_adj = jnp.dot(delta_bar, coefficients, preferred_element_type=jnp.float32)
    basis_adjoint = lax.psum(partial_adj, "trade").astype(jnp.bfloat16)
    return (margin_now.T, basis_adjoint)


def solution(mesh):
    placed = (
        P(("date", "path"), None),
        P(("date", "trade"), None),
        P("trade"),
        P("trade"),
        P(),
        P(),
        P("trade"),
    )
    whole = split_paths if mesh.shape["trade"] == 2 * DEEP else body
    return jax.shard_map(
        whole,
        mesh=mesh,
        in_specs=placed,
        out_specs=(P("trade", ("date", "path")), P(("date", "path"), None)),
        check_vma=False,
    )
```

```python
import functools
import jax
import jax.numpy as jnp
from jax import lax
from jax.experimental import pallas as pl
from jax.experimental.pallas import tpu as pltpu
from jax.sharding import PartitionSpec as P

MESH = pl.DeviceIdType.MESH
TERMS = 2
PIECES = 2
ADJ_PIECES = 4
DEEP = 4


def split_terms(value, count):
    parts = []
    for _ in range(count):
        head = value.astype(jnp.bfloat16)
        parts.append(head)
        value = value - head.astype(jnp.float32)
    return parts


def dot_nt(a, b):
    return lax.dot_general(a, b, (((1,), (1,)), ((), ())), preferred_element_type=jnp.float32)


def dot_nn(a, b):
    return jnp.dot(a, b, preferred_element_type=jnp.float32)


def margin_kernel(
    owners, basis_in, coef_in, cpty_in, bucket_in, rw_in, corr_in, spread_in,
    adj_out, margin_out,
    held, adj_ref, margin_ref, rows_buf, cpty_buf, bucket_buf, rw_buf, corr_buf, spread_buf,
    msg, msgs, gram, cols_buf, bucket_hot, cpty_hot, cpty_cols, bar_buf, msend, mrecv,
    local, zu, zd, zr, xs, xr, cs, cr, gs, gr, ms, mr, az_u, az_d, az_r, ax_s, ax_r, outs,
):
    t = lax.axis_index("trade")
    k = lax.axis_index("path")
    z = t // 2
    x = t % 2
    per_device, width = coef_in.shape
    half = per_device // 2
    span = width // PIECES
    adj_span = width // ADJ_PIECES
    buckets = corr_in.shape[0]
    trades = owners * per_device
    path_share = rows_buf.shape[0]
    cpty_dev = mrecv.shape[1]
    cptys = owners * cpty_dev
    code_lanes = -(-per_device // 128) * 128

    def slot(zz, xx, rz, rx):
        return (xx + rx) % 2 * 4 + (zz // 2 + rz // 2) % 2 * 2 + (zz + rz // 2) % 2

    def send(src, dst, send_sem, recv_sem, to_trade, to_path):
        return pltpu.make_async_remote_copy(
            src_ref=src, dst_ref=dst, send_sem=send_sem, recv_sem=recv_sem,
            device_id={"trade": to_trade, "path": to_path}, device_id_type=MESH,
        )

    own = slot(z, x, z, x)
    small = [
        pltpu.make_async_copy(cpty_in, cpty_buf, local.at[0]),
        pltpu.make_async_copy(bucket_in, bucket_buf, local.at[1]),
        pltpu.make_async_copy(spread_in, spread_buf, local.at[2]),
    ]
    shard = [
        pltpu.make_async_copy(
            coef_in.at[pl.ds(kk * half, half)], held.at[own * 2 + kk], local.at[3 + kk]
        )
        for kk in range(2)
    ]
    rest = [
        pltpu.make_async_copy(rw_in, rw_buf, local.at[5]),
        pltpu.make_async_copy(corr_in, corr_buf, local.at[6]),
        pltpu.make_async_copy(
            basis_in.at[pl.ds(pl.multiple_of(t * path_share, 16), path_share)], rows_buf, local.at[7]
        ),
    ]
    for copy in small + shard + rest:
        copy.start()

    barrier = pltpu.get_barrier_semaphore()
    for step in range(1, owners):
        pl.semaphore_signal(
            barrier, inc=1, device_id={"trade": (t + step) % owners, "path": k}, device_id_type=MESH
        )
    pl.semaphore_signal(barrier, inc=1, device_id={"trade": t, "path": 1 - k}, device_id_type=MESH)

    for copy in small:
        copy.wait()
    msg[...] = jnp.zeros_like(msg)
    msg[:, :per_device] = (cpty_buf[...] * buckets + bucket_buf[...]).astype(jnp.float32)
    msg[:, code_lanes:code_lanes + cpty_dev] = spread_buf[...]
    msgs[0] = msg[...]
    for copy in shard:
        copy.wait()
    pl.semaphore_wait(barrier, owners)

    def msg_copy(step):
        return send(msg, msgs.at[step], gs.at[step], gr.at[step], (t + step) % owners, k)

    def piece(where, p):
        return held.at[where * 2 + k, :, pl.ds(p * span, span)]

    def hop(zz, xx, p, sems, arrive, rz, rx):
        return send(
            piece(slot(zz, xx, z, x), p), piece(slot(zz, xx, rz, rx), p),
            sems.at[zz * PIECES + p], arrive.at[zz * PIECES + p], rz * 2 + rx, k,
        )

    def up(zz, p):
        return hop(zz, x, p, zu, zr, z + 1, x)

    def down(zz, p):
        return hop(zz, x, p, zd, zr, z - 1, x)

    def across(zz, p):
        return hop(zz, x, p, xs, xr, z, 1 - x)

    def over(where, p):
        ref = piece(where, p)
        sem = where * PIECES + p
        return send(ref, ref, cs.at[sem], cr.at[sem], t, 1 - k)

    def chain_arrived(zz, p):
        ref = piece(slot(zz, x, z, x), p)
        sem = zz * PIECES + p
        send(ref, ref, zu.at[sem], zr.at[sem], z * 2 + 1 - x, k).wait_recv()

    def across_arrived(zz, p):
        ref = piece(slot(zz, 1 - x, z, x), p)
        sem = zz * PIECES + p
        send(ref, ref, xs.at[sem], xr.at[sem], z * 2 + 1 - x, k).wait_recv()

    for p in range(PIECES):
        @pl.when(z < DEEP - 1)
        def _():
            up(z, p).start()

        @pl.when(z > 0)
        def _():
            down(z, p).start()

        across(z, p).start()
        if p == 0:
            for step in range(1, owners):
                msg_copy(step).start()

    def chain_arrival(j, p):
        @pl.when(z - j >= 0)
        def _():
            zz = z - j
            chain_arrived(zz, p)

            @pl.when(z < DEEP - 1)
            def _():
                up(zz, p).start()
            across(zz, p).start()
            over(slot(zz, x, z, x), p).start()

        @pl.when(z + j < DEEP)
        def _():
            zz = z + j
            chain_arrived(zz, p)

            @pl.when(z > 0)
            def _():
                down(zz, p).start()
            across(zz, p).start()
            over(slot(zz, x, z, x), p).start()

    def across_at(zz, p):
        across_arrived(zz, p)
        over(slot(zz, 1 - x, z, x), p).start()

    def across_arrival(j, p):
        if j == 0:
            across_at(z, p)
            return

        @pl.when(z - j >= 0)
        def _():
            across_at(z - j, p)

        @pl.when(z + j < DEEP)
        def _():
            across_at(z + j, p)

    for copy in rest:
        copy.wait()
    rw_rows = jnp.broadcast_to(rw_buf[...], (buckets, buckets))
    scaled = corr_buf[...] * rw_rows * rw_rows.T
    scaled_terms = jnp.concatenate(split_terms(scaled, TERMS), axis=1)

    chain_arrival(1, 0)
    chain_arrival(1, 1)
    for step in range(1, owners):
        msg_copy(step).wait_recv()

    def sender(i):
        zz = (i // 2 + z // 2) % 2 * 2 + (i + z // 2) % 2
        return zz * 2 + (i // 4 + x) % 2

    codes = jnp.concatenate(
        [msgs[(t - sender(i)) % owners][:, :per_device] for i in range(owners)], axis=1
    ).astype(jnp.int32)
    spread = jnp.concatenate(
        [msgs[(t - o) % owners][:, code_lanes:code_lanes + cpty_dev] for o in range(owners)], axis=1
    )
    cpty_row = codes // buckets
    bucket_row = codes % buckets
    bucket_hot[...] = (
        lax.broadcasted_iota(jnp.int32, (buckets, trades), 0) == bucket_row
    ).astype(jnp.float32).astype(jnp.bfloat16)
    cpty_hot[...] = (
        lax.broadcasted_iota(jnp.int32, (cptys, trades), 0) == cpty_row
    ).astype(jnp.float32).astype(jnp.bfloat16)
    cols_buf[...] = jnp.broadcast_to(codes.astype(jnp.float32), (8, trades)).T.astype(jnp.int32)

    block_rows = per_device

    def build(first, last):
        @pl.loop(first, last)
        def _(i):
            rows = pl.ds(pl.multiple_of(i * block_rows, 16), block_rows)
            code_col = cols_buf[rows, :1]
            hot = (
                lax.broadcasted_iota(jnp.int32, (block_rows, buckets), 1) == code_col % buckets
            ).astype(jnp.float32).astype(jnp.bfloat16)
            same = code_col // buckets == cpty_row
            cpty_cols[rows, :] = (
                lax.broadcasted_iota(jnp.int32, (block_rows, cptys), 1) == code_col // buckets
            ).astype(jnp.float32).astype(jnp.bfloat16)
            picked = dot_nn(hot, scaled_terms).astype(jnp.bfloat16)
            stacked = jnp.concatenate(
                [picked[:, term * buckets:(term + 1) * buckets] for term in range(TERMS)], axis=0
            )
            blocks = dot_nn(stacked, bucket_hot[...])
            for term in range(TERMS):
                block = blocks[term * block_rows:(term + 1) * block_rows]
                gram[term, rows, :] = jnp.where(same, block, 0.0).astype(jnp.bfloat16)

    def deltas(first, last):
        for where in range(first, last):
            for p in range(PIECES):
                if where < 2:
                    @pl.when(where != own)
                    def _():
                        over(where, p).wait_recv()
                else:
                    over(where, p).wait_recv()
        coef_rows = held[first * 2:last * 2].reshape((last - first) * per_device, width)
        return dot_nt(rows_buf[...], coef_rows)

    def spans_of(delta, first, last):
        out = dot_nn(delta, gram[TERMS - 1, first:last, :])
        for term in range(TERMS - 2, -1, -1):
            out = out + dot_nn(delta, gram[term, first:last, :])
        return out

    chain_arrival(2, 0)
    across_arrival(0, 0)
    across_arrival(0, 1)
    build(0, 1)
    chain_arrival(2, 1)
    build(1, 2)
    chain_arrival(3, 0)
    build(2, 3)
    chain_arrival(3, 1)
    across_arrival(1, 0)
    build(3, 4)
    across_arrival(1, 1)
    build(4, 6)
    across_arrival(2, 0)
    build(6, 8)
    across_arrival(2, 1)
    cut, tail = trades * 2 // 5, trades * 4 // 5
    d0 = deltas(0, 4)
    v = spans_of(d0[:, :cut].astype(jnp.bfloat16), 0, cut)
    d1 = deltas(4, 7)
    across_arrival(3, 0)
    middle = jnp.concatenate([d0[:, cut:], d1], axis=1)
    v = v + spans_of(middle[:, :tail - cut].astype(jnp.bfloat16), cut, tail)
    across_arrival(3, 1)
    d2 = deltas(7, 8)
    delta_all = jnp.concatenate([d0, d1, d2], axis=1).astype(jnp.bfloat16)
    v = v + spans_of(delta_all[:, tail:], tail, trades)
    delta_all = delta_all.astype(jnp.float32)

    terms = jnp.concatenate(split_terms(delta_all * v, 3), axis=0)
    sums = dot_nn(terms, cpty_cols[...])
    quad = sums[:path_share] + (sums[path_share:2 * path_share] + sums[2 * path_share:])
    margin = jnp.sqrt(quad + 1e-06)
    ratio_terms = jnp.concatenate(split_terms(spread / margin, 3), axis=0)
    spans = dot_nn(ratio_terms, cpty_hot[...])
    ratio = spans[:path_share] + (spans[path_share:2 * path_share] + spans[2 * path_share:])
    bar_buf[...] = (ratio * v).astype(jnp.bfloat16)

    def a_piece(zz, xx, p):
        return adj_ref.at[zz * 2 + xx, :, pl.ds(p * adj_span, adj_span)]

    def a_up(zz, p):
        ref = a_piece(zz, x, p)
        sem = zz * ADJ_PIECES + p
        return send(ref, ref, az_u.at[sem], az_r.at[sem], (z + 1) * 2 + x, k)

    def a_down(zz, p):
        ref = a_piece(zz, x, p)
        sem = zz * ADJ_PIECES + p
        return send(ref, ref, az_d.at[sem], az_r.at[sem], (z - 1) * 2 + x, k)

    def a_across(zz, xx, p):
        ref = a_piece(zz, xx, p)
        sem = zz * ADJ_PIECES + p
        return send(ref, ref, ax_s.at[sem], ax_r.at[sem], z * 2 + 1 - x, k)

    def out_copy(where):
        return pltpu.make_async_copy(adj_ref.at[where], adj_out.at[where], outs.at[where])

    for p in range(ADJ_PIECES):
        if p % (ADJ_PIECES // PIECES) == 0:
            wide = slice(p * adj_span, p * adj_span + span)
            coef_all = held[:, :, wide].reshape(trades, span)
            adj_ref[t, :, wide] = dot_nn(bar_buf[...], coef_all).astype(jnp.bfloat16)

        @pl.when(z < DEEP - 1)
        def _():
            a_up(z, p).start()

        @pl.when(z > 0)
        def _():
            a_down(z, p).start()

        a_across(z, x, p).start()
    out_copy(t).start()

    flipped = jnp.concatenate([margin, margin], axis=0).T[:, :path_share]
    msend[...] = flipped.reshape(owners, cpty_dev, path_share)

    def margin_copy(step):
        to = (t + step) % owners
        return send(msend.at[to], mrecv.at[step], ms.at[step], mr.at[step], to, k)

    for step in range(1, owners):
        margin_copy(step).start()

    for j in range(1, DEEP):
        for p in range(ADJ_PIECES):
            @pl.when(z - j >= 0)
            def _():
                a_up(z - j, p).wait_recv()

                @pl.when(z < DEEP - 1)
                def _():
                    a_up(z - j, p).start()
                a_across(z - j, x, p).start()

            @pl.when(z + j < DEEP)
            def _():
                a_down(z + j, p).wait_recv()

                @pl.when(z > 0)
                def _():
                    a_down(z + j, p).start()
                a_across(z + j, x, p).start()

        @pl.when(z - j >= 0)
        def _():
            out_copy((z - j) * 2 + x).start()

        @pl.when(z + j < DEEP)
        def _():
            out_copy((z + j) * 2 + x).start()

    for step in range(1, owners):
        margin_copy(step).wait_recv()
    mrecv[0] = msend[t]
    for first in range(0, owners, 2):
        pair = [mrecv[(t - o) % owners] for o in (first, first + 1)]
        margin_ref[:, first * path_share:(first + 2) * path_share] = jnp.concatenate(pair, axis=1)
    margin_done = pltpu.make_async_copy(margin_ref, margin_out, local.at[0])
    margin_done.start()

    def adj_across(zz):
        for p in range(ADJ_PIECES):
            a_across(zz, 1 - x, p).wait_recv()
        out_copy(zz * 2 + 1 - x).start()

    adj_across(z)
    for j in range(1, DEEP):
        @pl.when(z - j >= 0)
        def _():
            adj_across(z - j)

        @pl.when(z + j < DEEP)
        def _():
            adj_across(z + j)

    for step in range(1, owners):
        msg_copy(step).wait_send()
        margin_copy(step).wait_send()
    for p in range(PIECES):
        for where in range(owners):
            @pl.when(where != own)
            def _():
                over(where, p).wait_send()
        for zz in range(DEEP):
            across(zz, p).wait_send()

            @pl.when((zz <= z) & (z < DEEP - 1))
            def _():
                up(zz, p).wait_send()

            @pl.when((zz >= z) & (z > 0))
            def _():
                down(zz, p).wait_send()
    for p in range(ADJ_PIECES):
        for zz in range(DEEP):
            a_across(zz, x, p).wait_send()

            @pl.when((zz <= z) & (z < DEEP - 1))
            def _():
                a_up(zz, p).wait_send()

            @pl.when((zz >= z) & (z > 0))
            def _():
                a_down(zz, p).wait_send()
    margin_done.wait()
    for where in range(owners):
        out_copy(where).wait()


def hand_over(adj_in, margin_in, adj_out, margin_out, adj_held, margin_held, sems):
    count = adj_in.shape[0]
    legs = [(adj_in.at[i], adj_held.at[i], adj_out.at[i]) for i in range(count)]
    legs.append((margin_in, margin_held, margin_out))
    reads = [pltpu.make_async_copy(a, b, sems.at[i]) for i, (a, b, _) in enumerate(legs)]
    writes = [
        pltpu.make_async_copy(b, c, sems.at[count + 1 + i]) for i, (_, b, c) in enumerate(legs)
    ]
    for copy in reads:
        copy.start()
    for read, write in zip(reads, writes):
        read.wait()
        write.start()
    for copy in writes:
        copy.wait()


def split_paths(
    basis_values, coefficients, trade_cpty, trade_bucket, risk_weights, correlation, funding_spread
):
    owners = lax.axis_size("trade")
    per_device, width = coefficients.shape
    cpty_dev = funding_spread.shape[0]
    buckets = risk_weights.shape[0]
    path_rows = basis_values.shape[0]
    path_share = path_rows // owners
    trades = owners * per_device
    cptys = owners * cpty_dev
    hbm = pl.BlockSpec(memory_space=pltpu.HBM)
    dma = pltpu.SemaphoreType.DMA
    f32, i32, bf16 = jnp.float32, jnp.int32, jnp.bfloat16
    msg_lanes = -(-per_device // 128) * 128 + 128
    pieces = DEEP * PIECES
    adj_pieces = DEEP * ADJ_PIECES
    adj, margin = pl.pallas_call(
        functools.partial(margin_kernel, owners),
        out_shape=(
            jax.ShapeDtypeStruct((owners, path_share, width), bf16),
            jax.ShapeDtypeStruct((cpty_dev, path_rows), f32),
        ),
        in_specs=[hbm] * 7,
        out_specs=(hbm, hbm),
        scratch_shapes=[
            pltpu.VMEM((owners * 2, per_device // 2, width), bf16),
            pltpu.VMEM((owners, path_share, width), bf16),
            pltpu.VMEM((cpty_dev, path_rows), f32),
            pltpu.VMEM((path_share, width), bf16),
            pltpu.VMEM((1, per_device), i32),
            pltpu.VMEM((1, per_device), i32),
            pltpu.VMEM((1, buckets), f32),
            pltpu.VMEM((buckets, buckets), f32),
            pltpu.VMEM((1, cpty_dev), f32),
            pltpu.VMEM((1, msg_lanes), f32),
            pltpu.VMEM((owners, 1, msg_lanes), f32),
            pltpu.VMEM((TERMS, trades, trades), bf16),
            pltpu.VMEM((trades, 8), i32),
            pltpu.VMEM((buckets, trades), bf16),
            pltpu.VMEM((cptys, trades), bf16),
            pltpu.VMEM((trades, cptys), bf16),
            pltpu.VMEM((path_share, trades), bf16),
            pltpu.VMEM((owners, cpty_dev, path_share), f32),
            pltpu.VMEM((owners, cpty_dev, path_share), f32),
            dma((8,)), dma((pieces,)), dma((pieces,)), dma((pieces,)), dma((pieces,)), dma((pieces,)),
            dma((owners * PIECES,)), dma((owners * PIECES,)),
            dma((owners,)), dma((owners,)), dma((owners,)), dma((owners,)),
            dma((adj_pieces,)), dma((adj_pieces,)), dma((adj_pieces,)), dma((adj_pieces,)),
            dma((adj_pieces,)), dma((owners,)),
        ],
        compiler_params=pltpu.CompilerParams(
            collective_id=0, has_side_effects=True, vmem_limit_bytes=56 * 1024 * 1024
        ),
    )(
        basis_values, coefficients, trade_cpty[None, :], trade_bucket[None, :],
        risk_weights[None, :], correlation, funding_spread[None, :],
    )
    adj, margin = pl.pallas_call(
        hand_over,
        out_shape=(
            jax.ShapeDtypeStruct(adj.shape, bf16), jax.ShapeDtypeStruct(margin.shape, f32),
        ),
        in_specs=[hbm, hbm],
        out_specs=(hbm, hbm),
        scratch_shapes=[
            pltpu.VMEM(adj.shape, bf16), pltpu.VMEM(margin.shape, f32), dma((2 * owners + 2,)),
        ],
        compiler_params=pltpu.CompilerParams(vmem_limit_bytes=56 * 1024 * 1024),
    )(adj, margin)
    return (margin, adj.reshape(path_rows, width))


def margin_terms(arrived, got_codes, risk_weights, correlation, funding_spread):
    path_rows = arrived.shape[0]
    cpty_count = funding_spread.shape[0]
    bucket_count = risk_weights.shape[0]
    is_filled = got_codes >= 0
    column_ids = jnp.arange(cpty_count * bucket_count, dtype=jnp.int32)
    hot_table = (got_codes[:, None] == column_ids[None, :]).astype(jnp.bfloat16)
    bucket_sums = jnp.dot(arrived, hot_table, preferred_element_type=jnp.float32)
    weighted = (
        bucket_sums.reshape(path_rows, cpty_count, bucket_count) * risk_weights[None, None, :]
    )
    rho_w = jnp.einsum("pcb,db->pcd", weighted, correlation, precision=lax.Precision.HIGHEST)
    margin_now = jnp.sqrt(jnp.sum(weighted * rho_w, axis=2) + 1e-06)
    sens_bar = (
        funding_spread[None, :, None] * risk_weights[None, None, :] * rho_w / margin_now[:, :, None]
    )
    flat_bar = sens_bar.reshape(path_rows, cpty_count * bucket_count)
    safe_codes = jnp.where(is_filled, got_codes, 0)
    slot_bar = jnp.take(flat_bar, safe_codes, axis=1) * is_filled[None, :].astype(jnp.float32)
    return (margin_now, slot_bar.astype(jnp.bfloat16))


def body(
    basis_values, coefficients, trade_cpty, trade_bucket, risk_weights, correlation, funding_spread
):
    owners = lax.axis_size("trade")
    per_device = coefficients.shape[0]
    capacity = max(2, 2 * per_device // owners)
    slot_total = owners * capacity
    cpty_count = funding_spread.shape[0]
    bucket_count = risk_weights.shape[0]
    path_rows = basis_values.shape[0]
    owner_of = trade_cpty // cpty_count
    trade_code = trade_cpty % cpty_count * bucket_count + trade_bucket
    position = jnp.arange(per_device, dtype=jnp.int32)
    same_owner = owner_of[:, None] == owner_of[None, :]
    earlier = position[None, :] < position[:, None]
    rank_in = jnp.sum((same_owner & earlier).astype(jnp.int32), axis=1)
    slot_index = owner_of * capacity + rank_in
    codes_out = jnp.full((slot_total,), -1, jnp.int32).at[slot_index].set(trade_code)
    got_codes = lax.all_to_all(codes_out, "trade", split_axis=0, concat_axis=0, tiled=True)
    delta_rows = lax.dot_general(
        basis_values, coefficients, (((1,), (1,)), ((), ())), preferred_element_type=jnp.float32
    ).astype(jnp.bfloat16)
    outgoing = jnp.zeros((path_rows, slot_total), jnp.bfloat16).at[:, slot_index].set(delta_rows)
    arrived = lax.all_to_all(outgoing, "trade", split_axis=1, concat_axis=1, tiled=True)
    margin_now, slot_bar = margin_terms(
        arrived, got_codes, risk_weights, correlation, funding_spread
    )
    returned = lax.all_to_all(slot_bar, "trade", split_axis=1, concat_axis=1, tiled=True)
    delta_bar = returned[:, slot_index]
    partial_adj = jnp.dot(delta_bar, coefficients, preferred_element_type=jnp.float32)
    basis_adjoint = lax.psum(partial_adj, "trade").astype(jnp.bfloat16)
    return (margin_now.T, basis_adjoint)


def solution(mesh):
    placed = (
        P(("date", "path"), None),
        P(("date", "trade"), None),
        P("trade"),
        P("trade"),
        P(),
        P(),
        P("trade"),
    )
    whole = split_paths if mesh.shape["trade"] == 2 * DEEP else body
    return jax.shard_map(
        whole,
        mesh=mesh,
        in_specs=placed,
        out_specs=(P("trade", ("date", "path")), P(("date", "path"), None)),
        check_vma=False,
    )
```
